32 devices in a mesh: dp: 8 (over z, x), mp: 4 (over y, core).
Axes of the slice: x: 2, y: 2, z: 4, core: 2. Of those that a mesh axis runs over, the one named last changes fastest.
Arguments:
- inputs: bfloat16 [16384, 768], P(('dp', 'mp')), may hold values from -6 to 6
- cotangent: bfloat16 [16384, 768], P(('dp', 'mp')), may hold values from -6 to 6
- ln1_gain: float32 [768], replicated, may hold values from 0.1 to 1.9
- ln1_bias: float32 [768], replicated, may hold values from -3 to 3
- w_qkv: bfloat16 [3, 768, 768], P(None, None, 'mp'), may hold values from -0.21875 to 0.21875
- qv_bias: float32 [2, 768], P(None, 'mp'), may hold values from -3 to 3
- w_out: bfloat16 [768, 768], P('mp'), may hold values from -1.25 to 1.25
- out_bias: float32 [768], replicated, may hold values from -3 to 3
- ln2_gain: float32 [768], replicated, may hold values from 0.1 to 1.9
- ln2_bias: float32 [768], replicated, may hold values from -3 to 3
- w_fc: bfloat16 [768, 3072], P(None, 'mp'), may hold values from -0.21875 to 0.21875
- fc_bias: float32 [3072], P('mp'), may hold values from -3 to 3
- w_proj: bfloat16 [3072, 768], P('mp'), may hold values from -0.3125 to 0.3125
- proj_bias: float32 [768], replicated, may hold values from -3 to 3
- doc_lengths: int32 [16, 4], P('dp'), may hold values from 0 to 1024, as said below
Outputs:
- layer_out: bfloat16 [16384, 768], P(('dp', 'mp'))
- input_grad: bfloat16 [16384, 768], P(('dp', 'mp'))
- ln1_gain_grad: float32 [768], replicated
- ln1_bias_grad: float32 [768], replicated
- qkv_grad: float32 [3, 768, 768], P(None, None, 'mp')
- qv_bias_grad: float32 [2, 768], P(None, 'mp')
- out_weight_grad: float32 [768, 768], P('mp')
- out_bias_grad: float32 [768], replicated
- ln2_gain_grad: float32 [768], replicated
- ln2_bias_grad: float32 [768], replicated
- fc_weight_grad: float32 [768, 3072], P(None, 'mp')
- fc_bias_grad: float32 [3072], P('mp')
- proj_weight_grad: float32 [3072, 768], P('mp')
- proj_bias_grad: float32 [768], replicated
The draws below stay inside these ranges and needn't reach their ends.
Inputs may be any that keep to these rules, and one draw needn't show every extreme that they name: `doc_lengths`: each row lists the lengths of its packed documents in order, each 1 or more, then zeros; a row's lengths add up to between 973 and 1024, and positions past the sum are padding. Some row holds a single document of all 1024 positions.
All inputs are finite; a program needn't handle non-finite values.
Results may differ from the reference program's by a relative error of at most 0.017.
Values may be sent and summed in bfloat16 or wider, within the bound.
A program may use at most 128 MiB of HBM per device.

```python
import math
import jax
import jax.numpy as jnp
from jax import lax

D = 768
HEADS = 12
HD = 64
FF = 3072
SEQ = 1024
DOCS = 4
ROWS = 16
TOKENS = 16384


def draw_doc_lengths(key, part):
    key = jax.random.fold_in(key, 11)
    cut_key, pad_key, pick_key = jax.random.split(key, 3)
    span = SEQ - SEQ // 20 - 1

    def cut_row(row_key):
        return jnp.sort(jax.random.permutation(row_key, span)[:DOCS - 1] + 1)
    cuts = jax.vmap(cut_row)(jax.random.split(cut_key, ROWS)).astype(jnp.int32)
    padding = jax.random.randint(pad_key, (ROWS, 1), 0, SEQ // 20 + 1).astype(jnp.int32)
    bounds = jnp.concatenate([jnp.zeros((ROWS, 1), jnp.int32), cuts, (SEQ - padding).astype(jnp.int32)], axis=1)
    lengths = bounds[:, 1:] - bounds[:, :-1]
    chosen = jax.random.randint(pick_key, (), 0, ROWS)
    single = jnp.zeros((DOCS,), jnp.int32).at[0].set(SEQ)
    lengths = jnp.where((jnp.arange(ROWS) == chosen)[:, None], single[None, :], lengths)
    return lengths.astype(jnp.int32)


def strengthened(entries, stream_key, source, target, shards_of, factor):
    def block_of(position):
        return (jnp.arange(entries.shape[position]) // (entries.shape[position] // shards_of)).reshape((-1,) + (1,) * (entries.ndim - 1 - position))

    near = jax.random.permutation(stream_key, shards_of)[block_of(target)]
    second = (block_of(target) + shards_of // 2) % shards_of
    return jnp.where((block_of(source) == near) | (block_of(source) == second), factor * entries, entries)


def levels(key, shape, shards, smallest, largest):
    level, own = 1.0, jax.random.fold_in(key, 6)
    for axis_at, shards_of in shards:
        heights = jnp.exp(jax.random.uniform(jax.random.fold_in(own, axis_at), (shards_of,), jnp.float32, smallest / len(shards), largest / len(shards)))
        level = level * jnp.repeat(heights, shape[axis_at] // shards_of).reshape([-1 if axis == axis_at else 1 for axis in range(len(shape))])
    return level


def noise(key, dims, scale, most, cuts=(), kind=jnp.bfloat16):
    array = jax.random.normal(key, dims, jnp.float32) * scale
    if len(cuts) > 0:
        array = levels(key, dims, cuts, -0.22, 0.18) * array
    return jnp.clip(array, min=-most, max=most).astype(kind)


def gaussian_with(key, dims, deviation, bound, cuts, heavy, kind=jnp.bfloat16):
    array = deviation * jax.random.normal(key, dims, jnp.float32)
    if cuts:
        array = array * levels(key, dims, cuts, -0.22, 0.18)
    return jnp.clip(strengthened(array, jax.random.fold_in(key, 3), *heavy), -bound, bound).astype(kind)


def setup_inputs(seed: int = 0) -> dict:
    seeds = jax.random.split(jax.random.key(seed), 16)
    return {
        "inputs": noise(seeds[0], (TOKENS, D), 1.0, 6.0, ((0, 32),)),
        "cotangent": gaussian_with(seeds[1], (TOKENS, D), 1.0, 6.0, ((0, 32),), (0, 1, 32, 2.75)),
        "ln1_gain": jnp.clip(1.0 + 0.18 * jax.random.normal(seeds[2], (D,), jnp.float32), 0.1, 1.9),
        "ln1_bias": noise(seeds[3], (D,), 0.5, 3.0, (), jnp.float32),
        "w_qkv": noise(seeds[4], (3, D, D), D ** -0.5, 0.21875, ((2, 4),)),
        "qv_bias": noise(seeds[5], (2, D), 0.5, 3.0, ((1, 4),), jnp.float32),
        "w_out": noise(seeds[6], (D, D), (D // 32) ** -0.5, 1.25, ((0, 4),)),
        "out_bias": noise(seeds[7], (D,), 0.5, 3.0, (), jnp.float32),
        "ln2_gain": jnp.clip(1.0 + 0.18 * jax.random.normal(seeds[8], (D,), jnp.float32), 0.1, 1.9),
        "ln2_bias": noise(seeds[9], (D,), 0.5, 3.0, (), jnp.float32),
        "w_fc": noise(seeds[10], (D, FF), D ** -0.5, 0.21875, ((1, 4),)),
        "fc_bias": noise(seeds[11], (FF,), 0.5, 3.0, ((0, 4),), jnp.float32),
        "w_proj": noise(seeds[12], (FF, D), (FF // 8) ** -0.5, 0.3125, ((0, 4),)),
        "proj_bias": noise(seeds[13], (D,), 0.5, 3.0, (), jnp.float32),
        "doc_lengths": draw_doc_lengths(jax.random.fold_in(seeds[15], 71), 0),
    }


@jax.custom_vjp
def low(v):
    return lax.optimization_barrier(v.astype(jnp.bfloat16)).astype(jnp.float32)

@jax.custom_vjp
def low_back(v):
    return v

def low_keep(v):
    return (low(v), None)

def low_pass(kept, grad):
    return (grad,)

def back_keep(v):
    return (v, None)

def back_low(kept, grad):
    return (low(grad),)
low.defvjp(low_keep, low_pass)
low_back.defvjp(back_keep, back_low)
HIGHEST = lax.Precision.HIGHEST
branch_scale = 12 ** (-0.5)

def normalize(values, gain, shift):
    average = lax.optimization_barrier(jnp.mean(values, axis=-1, keepdims=True))
    centred = values - average
    spread = lax.optimization_barrier(jnp.mean(centred * centred, axis=-1, keepdims=True))
    return centred * lax.rsqrt(spread + 1e-05) * gain + shift

def segment_ids(lengths, length):
    ends = jnp.cumsum(lengths.astype(jnp.int32), axis=1).astype(jnp.int32)
    places = jnp.arange(length, dtype=jnp.int32)
    return lax.optimization_barrier(jnp.sum((places[None, :, None] >= ends[:, None, :]).astype(jnp.int32), axis=-1)).astype(jnp.int32)

def visible_keys(segments, docs):
    places = jnp.arange(segments.shape[0], dtype=jnp.int32)
    same = segments[:, None] == segments[None, :]
    causal = places[None, :] <= places[:, None]
    real = segments[None, :] < docs
    return same & causal & real | (places[:, None] == places[None, :])

def attend_row(row):
    queries, key_rows, value_rows, segments = row
    factor = 1.0 / math.sqrt(HD)
    raw = jnp.einsum('qhd,khd->hqk', queries, key_rows, precision=HIGHEST) * factor
    scores = low_back(raw)
    scores = jnp.where(visible_keys(segments, DOCS)[None], scores, -1e+30)
    peak = lax.optimization_barrier(jnp.max(scores, axis=-1, keepdims=True))
    exponent = jnp.exp(scores - peak)
    probs = exponent / lax.optimization_barrier(jnp.sum(exponent, axis=-1, keepdims=True))
    return jnp.einsum('hqk,khd->qhd', low(probs), value_rows, precision=HIGHEST)

def layer(state, gain1, shift1, weight_qkv, bias_qv, weight_out, bias_out, gain2, shift2, weight_fc, bias_fc, weight_proj, bias_proj, segments):
    normed1 = low(normalize(state, gain1, shift1))
    projected = jnp.einsum('td,cde->cte', normed1, weight_qkv, precision=HIGHEST)
    queries = low_back(low(projected[0] + bias_qv[0]))
    key_rows = low_back(low(projected[1]))
    value_rows = low_back(low(projected[2] + bias_qv[1]))
    shape4 = (ROWS, SEQ, HEADS, HD)
    mixed = lax.map(jax.checkpoint(attend_row), (queries.reshape(shape4), key_rows.reshape(shape4), value_rows.reshape(shape4), segments))
    mixed = low_back(low(mixed.reshape(TOKENS, D)))
    attn = low_back(jnp.dot(mixed, weight_out, precision=HIGHEST))
    hidden = state + branch_scale * (attn + bias_out)
    normed2 = low(normalize(hidden, gain2, shift2))
    pre_act = low_back(jnp.dot(normed2, weight_fc, precision=HIGHEST)) + bias_fc
    activ = low(jax.nn.gelu(pre_act, approximate=True))
    mlp = low_back(jnp.dot(activ, weight_proj, precision=HIGHEST))
    return hidden + branch_scale * (mlp + bias_proj)

def reference(inputs, cotangent, ln1_gain, ln1_bias, w_qkv, qv_bias, w_out, out_bias, ln2_gain, ln2_bias, w_fc, fc_bias, w_proj, proj_bias, doc_lengths):
    segments = segment_ids(doc_lengths, SEQ)
    params = (inputs.astype(jnp.float32), ln1_gain.astype(jnp.float32), ln1_bias.astype(jnp.float32), w_qkv.astype(jnp.float32), qv_bias.astype(jnp.float32), w_out.astype(jnp.float32), out_bias.astype(jnp.float32), ln2_gain.astype(jnp.float32), ln2_bias.astype(jnp.float32), w_fc.astype(jnp.float32), fc_bias.astype(jnp.float32), w_proj.astype(jnp.float32), proj_bias.astype(jnp.float32))

    def forward(*values):
        return layer(*values, segments)
    result, pullback = jax.vjp(forward, *params)
    grads = pullback(cotangent.astype(jnp.float32))
    return (result.astype(jnp.bfloat16), grads[0].astype(jnp.bfloat16), grads[1], grads[2], grads[3], grads[4], grads[5], grads[6], grads[7], grads[8], grads[9], grads[10], grads[11], grads[12])
```

```python
import functools
import math

import jax
import jax.numpy as jnp
from jax import lax
from jax.experimental import pallas as pl
from jax.experimental.pallas import tpu as pltpu
from jax.sharding import PartitionSpec as P

HD = 64
SCALE = 12 ** (-0.5)
MESH = pl.DeviceIdType.MESH
F32 = jnp.float32
BF16 = jnp.bfloat16
NN = (((1,), (0,)), ((), ()))
NT = (((1,), (1,)), ((), ()))
TN = (((0,), (0,)), ((), ()))
BLOCK = 256
CHUNKS = 6
LN1G, LN1B, OUTB, LN2G, LN2B, PROJB, FCB, QVB = range(8)


def dot(a, b, dims=NN):
    return lax.dot_general(a, b, dims, preferred_element_type=F32)


def rows_of(start, size, align=16):
    return pl.ds(pl.multiple_of(start, align), size)


def centre(values):
    average = jnp.mean(values, axis=-1, keepdims=True)
    centred = values - average
    spread = jnp.mean(centred * centred, axis=-1, keepdims=True)
    rate = lax.rsqrt(spread + 1e-05)
    return centred * rate, rate


def block_kernel(
    x_ref, cot_ref, g1, b1, wqkv_hbm, qvb, wout_hbm, ob, g2, b2, wfc_hbm, fcb, wproj_hbm, pb, docs,
    layer_out, input_grad, grads, small_out,
    wqkv, wout, wfc, wproj, qvb_o, fcb_o, n1, n2, mg, ag, qh, kh, vh, mxh, mgh, p0, p1, p2, p3,
    s0, s1, s2, s3, act_t, plo, hid, hg, send_a, send_b, r_attn, r_mlp, r_n2,
    g_own, g_oth, y_in, x_in, z_in, piece, lo, sm_a, sm_b, sm_c, sm_d, sm_rc, sm_ry, sm_rx, sm_rz,
    cs, cr, ws, wr, fs, fr, ls, ys, yr, xs, xr, zs, zr, gs, gr, es, er, ks,
):
    half, width = x_ref.shape
    rows = 2 * half
    shard = wout_hbm.shape[0]
    nh = shard // HD
    hidden = wproj_hbm.shape[0]
    nblk = rows // BLOCK
    dp, mp = lax.axis_index("dp"), lax.axis_index("mp")
    core, y = lax.rem(mp, 2), lax.div(mp, 2)
    xi = lax.rem(dp, 2)
    zi = lax.rem(lax.div(dp, 2), 4)
    base = dp - 2 * zi
    core_id = (dp, mp + 1 - 2 * core)
    y_id = (dp, mp + 2 - 4 * y)
    x_id = (dp + 1 - 2 * xi, mp)

    def z_id(d):
        return (base + 2 * lax.rem(zi + d, 4), mp)

    mine, theirs = core * half, (1 - core) * half
    probs, scores_grad = (p0, p1, p2, p3), (s0, s1, s2, s3)

    def remote(src, dst, send, recv, target):
        return pltpu.make_async_remote_copy(
            src_ref=src, dst_ref=dst, send_sem=send, recv_sem=recv, device_id=target, device_id_type=MESH
        )

    def to_core(i, src, dst):
        return remote(src, dst, cs.at[i], cr.at[i], core_id)

    barrier = pltpu.get_barrier_semaphore()
    for target in (core_id, y_id, x_id, z_id(1), z_id(2), z_id(3)):
        pl.semaphore_signal(barrier, inc=1, device_id=target, device_id_type=MESH)
    pl.semaphore_wait(barrier, 6)

    def views(ref, lead, i, part):
        if i < 3:
            return ref.at[(*lead, i, rows_of(part * (shard // 2), shard // 2))]
        if i == 3:
            return ref.at[(*lead, rows_of(part * (shard // 2), shard // 2))]
        quarter = width // 4
        return ref.at[(*lead, rows_of(part * 2 * quarter + ((i - 4) % 2) * quarter, quarter))]

    def buffers(i):
        if i < 3:
            return wqkv_hbm, wqkv
        if i == 3:
            return wout_hbm, wout
        return (wfc_hbm, wfc) if i < 6 else (wproj_hbm, wproj)

    def weight_y(i):
        hbm, vmem = buffers(i)
        return remote(views(hbm, (), i, xi), views(vmem, (1,), i, xi), ws.at[i], wr.at[i], y_id)

    def weight_x(i):
        vmem = buffers(i)[1]
        return remote(views(vmem, (1,), i, xi), views(vmem, (1,), i, xi), fs.at[i], fr.at[i], x_id)

    def weight_own(i):
        hbm, vmem = ((wqkv_hbm, wqkv), (wout_hbm, wout), (wfc_hbm, wfc), (wproj_hbm, wproj))[i]
        return pltpu.make_async_copy(hbm, vmem.at[0], ls.at[i])

    copy_qvb = remote(qvb, qvb_o, ws.at[8], wr.at[8], y_id)
    copy_fcb = remote(fcb, fcb_o, ws.at[9], wr.at[9], y_id)

    def forward(i):
        weight_y(i).wait_recv()
        weight_x(i).start()

    weight_own(0).start()
    copy_qvb.start()
    for i in range(8):
        weight_y(i).start()
    copy_fcb.start()
    for i in range(1, 4):
        weight_own(i).start()

    def n1_copy(i):
        view = n1.at[rows_of(mine + i * BLOCK, BLOCK)]
        return to_core(i, view, view)

    for i in range(half // BLOCK):
        here = pl.ds(i * BLOCK, BLOCK)
        normal, _ = centre(x_ref[here, :].astype(F32))
        n1[rows_of(mine + i * BLOCK, BLOCK), :] = (normal * g1[...] + b1[...]).astype(BF16)
        n1_copy(i).start()
    mg_copy = to_core(2, mg.at[rows_of(mine, half)], mg.at[rows_of(mine, half)])
    total = jnp.zeros((1, width), F32)
    for i in range(half // BLOCK):
        here = pl.ds(i * BLOCK, BLOCK)
        values = cot_ref[here, :].astype(F32)
        mg[rows_of(mine + i * BLOCK, BLOCK), :] = (SCALE * values).astype(BF16)
        total = total + jnp.sum(values, axis=0, keepdims=True)
    mg_copy.start()
    sm_a[...] = jnp.zeros_like(sm_a)
    sm_a[pl.ds(PROJB, 1), :] = SCALE * total

    place = lax.broadcasted_iota(jnp.int32, (rows, 1), 0)
    first = jnp.zeros((rows, 1), jnp.int32)
    end = 0
    slots = docs.shape[1]
    for i in range(slots):
        end = end + docs[y, i]
        first = jnp.where(place >= end, place if i == slots - 1 else end, first)
    lo[...] = first

    def project(s, start, blocks):
        bias = qvb if s == 0 else qvb_o

        def body(m, _):
            here = rows_of(start + m * BLOCK, BLOCK)
            tokens = n1[here, :]
            for j, out in enumerate((qh, kh, vh)):
                t = dot(tokens, wqkv[s, j], NT)
                if j == 0:
                    t = (t + bias[pl.ds(0, 1), :]) * (1.0 / math.sqrt(HD))
                elif j == 2:
                    t = t + bias[pl.ds(1, 1), :]
                t = t.astype(BF16)
                for h in range(nh):
                    out[s * nh + h, here, :] = t[:, h * HD:(h + 1) * HD]
            return 0

        lax.fori_loop(0, blocks, body, 0)

    def attend(s, service):
        def head(t, _):
            service(t)
            h = s * nh + t
            for i in range(nblk):
                seen = BLOCK * (i + 1)
                here = pl.ds(BLOCK * i, BLOCK)
                score = dot(qh[h, here, :], kh[h, pl.ds(0, seen), :], NT)
                key = lax.broadcasted_iota(jnp.int32, (BLOCK, seen), 1)
                query = lax.broadcasted_iota(jnp.int32, (BLOCK, seen), 0) + BLOCK * i
                score = jnp.where((key >= lo[here, :]) & (key <= query), score, -1e30)
                peak = jnp.max(score, axis=-1, keepdims=True)
                exponent = jnp.exp(score - peak)
                scale = 1.0 / jnp.sum(exponent, axis=-1, keepdims=True)
                low = (exponent * scale).astype(BF16)
                probs[i][h] = low
                mxh[h, here, :] = dot(low, vh[h, pl.ds(0, seen), :]).astype(BF16)
            return 0

        lax.fori_loop(0, nh, head, 0)

    weight_own(0).wait()
    project(0, mine, half // BLOCK)
    for i in range(half // BLOCK):
        n1_copy(i).wait_recv()
    project(0, theirs, half // BLOCK)

    def service0(t):
        for i in range(3):
            @pl.when(t == i)
            def _():
                forward(i)

    attend(0, service0)
    copy_qvb.wait_recv()
    forward(3)
    for i in range(3):
        weight_x(i).wait_recv()
    project(1, 0, rows // BLOCK)

    def service1(t):
        for i in range(3):
            @pl.when(t == i)
            def _():
                forward(4 + i)

    attend(1, service1)

    weight_own(1).wait()
    weight_x(3).wait_recv()

    def mixed_of(s, here):
        return jnp.concatenate([mxh[s * nh + h, here, :] for h in range(nh)], axis=1)

    def attn_out(here):
        return dot(mixed_of(0, here), wout[0]) + dot(mixed_of(1, here), wout[1])

    attn_copy = to_core(3, send_a, r_attn)

    def attn_theirs(m, _):
        send_a[rows_of(m * BLOCK, BLOCK), :] = attn_out(rows_of(theirs + m * BLOCK, BLOCK)).astype(BF16)
        return 0

    def attn_mine(m, _):
        here = rows_of(m * BLOCK, BLOCK)
        part = attn_out(rows_of(mine + m * BLOCK, BLOCK))
        hid[here, :] = x_ref[here, :].astype(F32) + SCALE * (part + ob[...])
        return 0

    lax.fori_loop(0, half // BLOCK, attn_theirs, 0)
    attn_copy.start()
    lax.fori_loop(0, half // BLOCK, attn_mine, 0)
    attn_copy.wait()

    def n2_copy(i):
        view = n2.at[rows_of(mine + i * BLOCK, BLOCK)]
        return to_core(4 + i, view, view)

    for i in range(half // BLOCK):
        here = pl.ds(i * BLOCK, BLOCK)
        state = hid[here, :] + SCALE * r_attn[here, :].astype(F32)
        hid[here, :] = state
        normal, _ = centre(state)
        n2[rows_of(mine + i * BLOCK, BLOCK), :] = (normal * g2[...] + b2[...]).astype(BF16)
        n2_copy(i).start()

    def feed(s):
        bias = fcb if s == 0 else fcb_o
        a, b = math.sqrt(2 / math.pi), math.sqrt(2 / math.pi) * 0.044715

        def tile(f, _):
            cols = rows_of(f * BLOCK, BLOCK, BLOCK)
            total = jnp.zeros((1, BLOCK), F32)
            for m in range(2):
                here = pl.ds(half * m, half)
                u = dot(n2[here, :], wfc[s, :, cols]) + bias[:, cols]
                up = dot(mg[here, :], wproj[s, cols, :], NT)
                square = u * u
                th = jnp.tanh(u * (a + b * square))
                low = 0.5 + 0.5 * th
                act_t[s, cols, here] = (u * low).astype(BF16).T
                back = up * (low + (0.5 * u) * (1.0 - th * th) * (a + 3.0 * b * square))
                plo[s, here, cols] = back.astype(BF16)
                total = total + jnp.sum(back, axis=0, keepdims=True)
            sm_a[pl.ds(FCB + 8 * s, 1), cols] = total
            return 0

        lax.fori_loop(0, hidden // BLOCK, tile, 0)

    def grad_proj(s, out):
        def tile(n, _):
            cols = rows_of(n * BLOCK, BLOCK, BLOCK)
            out[pl.ds(0, hidden), cols] = dot(act_t[s], mg[:, cols]).astype(BF16)
            return 0

        lax.fori_loop(0, width // BLOCK, tile, 0)

    def grad_fc(s, out):
        def tile(n, _):
            cols = rows_of(n * BLOCK, BLOCK, BLOCK)
            out[rows_of(hidden + n * BLOCK, BLOCK), :] = dot(plo[s, :, cols], n2[...], TN).astype(BF16)
            return 0

        lax.fori_loop(0, hidden // BLOCK, tile, 0)

    chunk = (2 * hidden + 4 * shard) // CHUNKS
    part, bit = chunk // 2, chunk // 8

    def y_copy(k):
        here = rows_of(k * chunk, chunk)
        there = rows_of(lax.rem(k, 4) * chunk, chunk)
        return remote(g_oth.at[there], y_in.at[here], ys.at[k], yr.at[k], y_id)

    def x_copy(k):
        src = g_own.at[rows_of(k * chunk + (1 - xi) * part, part)]
        return remote(src, x_in.at[rows_of(k * part, part)], xs.at[k], xr.at[k], x_id)

    def z_copy(k, d):
        src = g_own.at[rows_of(k * chunk + xi * part + lax.rem(zi + d, 4) * bit, bit)]
        return remote(src, z_in.at[d - 1, rows_of(k * bit, bit)], zs.at[d - 1, k], zr.at[d - 1, k], z_id(d))

    def place_of(k):
        return grads.at[rows_of(k * chunk + xi * part + zi * bit, bit)]

    def g_copy(k, d):
        src = piece.at[rows_of(k * bit, bit)]
        return remote(src, place_of(k), gs.at[d - 1, k], gr.at[d - 1, k], z_id(d))

    def keep_copy(k):
        return pltpu.make_async_copy(piece.at[rows_of(k * bit, bit)], place_of(k), ks.at[k])

    def e_copy(k):
        view = grads.at[rows_of(k * chunk + xi * part, part)]
        return remote(view, view, es.at[k], er.at[k], x_id)

    def y_done(k):
        y_copy(k).wait_recv()
        step = part // 2

        def add(m, _):
            here = rows_of(k * chunk + m * step, step)
            g_own[here, :] = (g_own[here, :].astype(F32) + y_in[here, :].astype(F32)).astype(BF16)
            return 0

        lax.fori_loop(0, 4, add, 0)
        x_copy(k).start()

    def x_done(k):
        x_copy(k).wait_recv()
        step = part // 2

        def add(m, _):
            here = rows_of(k * chunk + xi * part + m * step, step)
            there = rows_of(k * part + m * step, step)
            g_own[here, :] = (g_own[here, :].astype(F32) + x_in[there, :].astype(F32)).astype(BF16)
            return 0

        lax.fori_loop(0, 2, add, 0)
        for d in (2, 1, 3):
            z_copy(k, d).start()

    def z_done(k):
        for d in (1, 2, 3):
            z_copy(k, d).wait_recv()
        there = rows_of(k * bit, bit)
        total = g_own[rows_of(k * chunk + xi * part + zi * bit, bit), :].astype(F32)
        for d in range(3):
            total = total + z_in[d, there, :].astype(F32)
        piece[there, :] = total.astype(BF16)
        keep_copy(k).start()
        for d in (2, 1, 3):
            g_copy(k, d).start()

    def g_done(k):
        keep_copy(k).wait()
        for d in (1, 2, 3):
            g_copy(k, d).wait_recv()
        e_copy(k).start()

    for i in range(half // BLOCK):
        n2_copy(i).wait_recv()
    mg_copy.wait_recv()
    weight_own(2).wait()
    weight_own(3).wait()
    feed(0)
    forward(7)
    grad_proj(0, g_own)
    grad_fc(0, g_own)
    copy_fcb.wait_recv()
    for i in range(4, 8):
        weight_x(i).wait_recv()
    feed(1)
    grad_proj(1, g_oth)
    y_copy(0).start()
    y_copy(1).start()

    def norm2_part(here, cols):
        return dot(plo[0, here, :], wfc[0, cols, :], NT) + dot(plo[1, here, :], wfc[1, cols, :], NT)

    def norm2_theirs(n, _):
        cols = rows_of(n * BLOCK, BLOCK, BLOCK)
        send_a[:, cols] = norm2_part(rows_of(theirs, half), cols).astype(BF16)
        return 0

    def norm2_mine(n, _):
        cols = rows_of(n * BLOCK, BLOCK, BLOCK)
        hg[:, cols] = norm2_part(rows_of(mine, half), cols)
        return 0

    norm2_copy = to_core(7, send_a, r_n2)
    lax.fori_loop(0, width // BLOCK, norm2_theirs, 0)
    norm2_copy.start()
    lax.fori_loop(0, width // BLOCK, norm2_mine, 0)
    grad_fc(1, g_oth)
    y_copy(2).start()
    y_copy(3).start()
    norm2_copy.wait()

    def ag_copy(i):
        view = ag.at[rows_of(mine + i * BLOCK, BLOCK)]
        return to_core(8 + i, view, view)

    def norm_back(grad, gain, normal, rate):
        n = grad * gain
        return rate * (
            n - jnp.mean(n, axis=-1, keepdims=True) - normal * jnp.mean(n * normal, axis=-1, keepdims=True)
        )

    sums = [jnp.zeros((1, width), F32) for _ in range(3)]
    for i in range(half // BLOCK):
        here = pl.ds(i * BLOCK, BLOCK)
        grad = hg[here, :] + r_n2[here, :].astype(F32)
        normal, rate = centre(hid[here, :])
        state_grad = cot_ref[here, :].astype(F32) + norm_back(grad, g2[...], normal, rate)
        hg[here, :] = state_grad
        ag[rows_of(mine + i * BLOCK, BLOCK), :] = (SCALE * state_grad).astype(BF16)
        ag_copy(i).start()
        for j, value in enumerate((grad * normal, grad, SCALE * state_grad)):
            sums[j] = sums[j] + jnp.sum(value, axis=0, keepdims=True)
    sm_a[pl.ds(LN2G, 1), :] = sums[0]
    sm_a[pl.ds(LN2B, 1), :] = sums[1]
    sm_a[pl.ds(OUTB, 1), :] = sums[2]

    def mlp_part(here, cols):
        return dot(act_t[0, :, here], wproj[0, :, cols], TN) + dot(act_t[1, :, here], wproj[1, :, cols], TN)

    def mlp_theirs(n, _):
        cols = rows_of(n * BLOCK, BLOCK, BLOCK)
        send_b[:, cols] = mlp_part(rows_of(theirs, half, BLOCK), cols).astype(BF16)
        return 0

    def mlp_mine(n, _):
        cols = rows_of(n * BLOCK, BLOCK, BLOCK)
        hid[:, cols] = hid[:, cols] + SCALE * (mlp_part(rows_of(mine, half, BLOCK), cols) + pb[:, cols])
        return 0

    mlp_copy = to_core(6, send_b, r_mlp)
    lax.fori_loop(0, width // BLOCK, mlp_theirs, 0)
    mlp_copy.start()
    lax.fori_loop(0, width // BLOCK, mlp_mine, 0)

    def mixed_grad(start):
        def body(m, _):
            here = rows_of(start + m * BLOCK, BLOCK)
            tokens = ag[here, :]
            for s in range(2):
                t = dot(tokens, wout[s], NT).astype(BF16)
                for h in range(nh):
                    mgh[s * nh + h, here, :] = t[:, h * HD:(h + 1) * HD]
            return 0

        lax.fori_loop(0, half // BLOCK, body, 0)

    mixed_grad(mine)
    for i in range(half // BLOCK):
        ag_copy(i).wait_recv()
    mixed_grad(theirs)

    def grad_out(s, out, start):
        def tile(n, _):
            cols = rows_of(n * BLOCK, BLOCK, BLOCK)
            mixed = mixed_of(s, slice(None))
            out[pl.ds(start, shard), cols] = dot(mixed, ag[:, cols], TN).astype(BF16)
            return 0

        lax.fori_loop(0, width // BLOCK, tile, 0)

    y_copy(0).wait_send()
    y_copy(1).wait_send()
    grad_out(1, g_oth, 0)
    grad_out(0, g_own, 2 * hidden)
    mlp_copy.wait()
    for i in range(half // BLOCK):
        n2_copy(i).wait_send()
        here = pl.ds(i * BLOCK, BLOCK)
        there = rows_of(mine + i * BLOCK, BLOCK)
        n2[there, :] = (hid[here, :] + SCALE * r_mlp[here, :].astype(F32)).astype(BF16)
    result = pltpu.make_async_copy(n2.at[rows_of(mine, half)], layer_out, ks.at[CHUNKS])
    result.start()

    def attend_back(s, service):
        def head(t, _):
            service(t)
            h = s * nh + t
            grad_t, query_t = mgh[h].T, qh[h].T
            for i in range(nblk):
                seen = BLOCK * (i + 1)
                here = pl.ds(BLOCK * i, BLOCK)
                d = mgh[h, here, :]
                inner = jnp.sum(d.astype(F32) * mxh[h, here, :].astype(F32), axis=-1, keepdims=True)
                prob_grad = dot(d, vh[h, pl.ds(0, seen), :], NT)
                ds = (probs[i][h].astype(F32) * (prob_grad - inner)).astype(BF16)
                scores_grad[i][...] = ds
                dq = dot(ds, kh[h, pl.ds(0, seen), :]) * (1.0 / math.sqrt(HD))
                act_t[s, rows_of(t * HD, HD), here] = dq.astype(BF16).T
            for j in range(nblk):
                cols = pl.ds(BLOCK * j, BLOCK)
                value_grad = key_grad = 0.0
                for i in range(j, nblk):
                    there = slice(BLOCK * i, BLOCK * (i + 1))
                    value_grad = value_grad + dot(grad_t[:, there], probs[i][h, :, cols])
                    key_grad = key_grad + dot(query_t[:, there], scores_grad[i][:, cols])
                act_t[s, rows_of(shard + t * HD, HD), cols] = key_grad.astype(BF16)
                act_t[s, rows_of(2 * shard + t * HD, HD), cols] = value_grad.astype(BF16)
            return 0

        lax.fori_loop(0, nh, head, 0)

    def grad_qkv(s, out, start):
        def tile(n, _):
            cols = rows_of(n * BLOCK, BLOCK, BLOCK)
            product = dot(act_t[s, pl.ds(0, 3 * shard), :], n1[:, cols])
            out[pl.ds(start + shard, 3 * shard), cols] = product.astype(BF16)
            return 0

        lax.fori_loop(0, width // BLOCK, tile, 0)

    def service2(t):
        @pl.when(t == 1)
        def _():
            y_done(0)

    attend_back(1, service2)
    grad_qkv(1, g_oth, 0)
    y_copy(4).start()
    y_copy(5).start()

    def service3(t):
        @pl.when(t == 0)
        def _():
            y_done(1)
            x_done(0)

        @pl.when(t == 2)
        def _():
            z_done(0)
            x_done(1)

    attend_back(0, service3)
    grad_qkv(0, g_own, 2 * hidden)

    def norm1_part(here, first):
        total = None
        for s in range(2):
            for j in range(3):
                t = act_t[s, pl.ds(j * shard, shard), here].T
                if j != 1:
                    cols = pl.ds(0 if j == 0 else BLOCK, shard)
                    line = pl.ds(QVB + 8 * s, 1)
                    sm_a[line, cols] = sm_a[line, cols] + jnp.sum(t.astype(F32), axis=0, keepdims=True)
                product = dot(t, wqkv[s, j])
                total = product if total is None else total + product
        return total

    def norm1_theirs(m, _):
        here = rows_of(theirs + m * BLOCK, BLOCK, BLOCK)
        send_b[rows_of(m * BLOCK, BLOCK), :] = norm1_part(here, m == 0).astype(BF16)
        return 0

    def norm1_mine(m, _):
        here = rows_of(mine + m * BLOCK, BLOCK, BLOCK)
        hid[rows_of(m * BLOCK, BLOCK), :] = norm1_part(here, False)
        return 0

    norm1_copy = to_core(10, send_b, r_attn)
    lax.fori_loop(0, half // BLOCK, norm1_theirs, 0)
    norm1_copy.start()
    lax.fori_loop(0, half // BLOCK, norm1_mine, 0)
    y_done(2)
    norm1_copy.wait()
    sums = [jnp.zeros((1, width), F32) for _ in range(2)]
    for i in range(half // BLOCK):
        here = pl.ds(i * BLOCK, BLOCK)
        grad = hid[here, :] + r_attn[here, :].astype(F32)
        normal, rate = centre(x_ref[here, :].astype(F32))
        input_grad[here, :] = (hg[here, :] + norm_back(grad, g1[...], normal, rate)).astype(BF16)
        sums[0] = sums[0] + jnp.sum(grad * normal, axis=0, keepdims=True)
        sums[1] = sums[1] + jnp.sum(grad, axis=0, keepdims=True)
    sm_a[pl.ds(LN1G, 1), :] = sums[0]
    sm_a[pl.ds(LN1B, 1), :] = sums[1]

    small_core = to_core(11, sm_a.at[pl.ds(0, 8)], sm_rc)
    small_core.start()
    y_done(3)
    x_done(2)
    z_done(1)
    g_done(0)
    small_core.wait()
    shared = lax.broadcasted_iota(jnp.int32, (8, width), 0) < FCB
    own, other = sm_a[pl.ds(0, 8), :], sm_a[pl.ds(8, 8), :]
    both = own + sm_rc[...]
    sm_b[pl.ds(0, 8), :] = jnp.where(shared, both, own)
    sm_b[pl.ds(8, 8), :] = jnp.where(shared, both, other)
    small_y = remote(sm_b.at[pl.ds(8, 8)], sm_ry, cs.at[12], cr.at[12], y_id)
    small_y.start()
    y_done(4)
    x_done(3)
    z_done(2)
    g_done(1)
    small_y.wait()
    sm_c[...] = sm_b[pl.ds(0, 8), :] + sm_ry[...]
    small_x = remote(sm_c, sm_rx, cs.at[13], cr.at[13], x_id)
    small_x.start()
    y_done(5)
    x_done(4)
    z_done(3)
    g_done(2)
    small_x.wait()
    sm_d[...] = sm_c[...] + sm_rx[...]
    small_z = [remote(sm_d, sm_rz.at[zi], cs.at[13 + d], cr.at[13 + d], z_id(d)) for d in (1, 2, 3)]
    for copy in small_z:
        copy.start()
    sm_rz[zi] = sm_d[...]
    x_done(5)
    z_done(4)
    g_done(3)
    z_done(5)
    g_done(4)
    for copy in small_z:
        copy.wait()
    small_out[...] = ((sm_rz[0] + sm_rz[1]) + sm_rz[2]) + sm_rz[3]
    g_done(5)

    for k in range(CHUNKS):
        e_copy(k).wait()
        if k > 1:
            y_copy(k).wait_send()
        x_copy(k).wait_send()
        for d in (1, 2, 3):
            z_copy(k, d).wait_send()
            g_copy(k, d).wait_send()
    for i in range(8):
        weight_y(i).wait_send()
        weight_x(i).wait_send()
    copy_qvb.wait_send()
    copy_fcb.wait_send()
    mg_copy.wait_send()
    for i in range(half // BLOCK):
        n1_copy(i).wait_send()
        ag_copy(i).wait_send()
    result.wait()


def shards(
    inputs, cotangent, ln1_gain, ln1_bias, w_qkv, qv_bias, w_out, out_bias, ln2_gain, ln2_bias,
    w_fc, fc_bias, w_proj, proj_bias, doc_lengths,
):
    half, width = inputs.shape
    rows = 2 * half
    shard = w_out.shape[0]
    heads = 2 * (shard // HD)
    hidden = w_proj.shape[0]
    total = 2 * hidden + 4 * shard
    nblk = rows // BLOCK
    vmem = pl.BlockSpec(memory_space=pltpu.VMEM)
    hbm = pl.BlockSpec(memory_space=pl.ANY)
    smem = pl.BlockSpec(memory_space=pltpu.SMEM)

    def low(*shape):
        return pltpu.VMEM(shape, BF16)

    def full(*shape):
        return pltpu.VMEM(shape, F32)

    dma = pltpu.SemaphoreType.DMA
    outs = pl.pallas_call(
        block_kernel,
        out_shape=(
            jax.ShapeDtypeStruct((half, width), BF16),
            jax.ShapeDtypeStruct((half, width), BF16),
            jax.ShapeDtypeStruct((total, width), BF16),
            jax.ShapeDtypeStruct((8, width), F32),
        ),
        in_specs=[vmem, vmem, vmem, vmem, hbm, vmem, hbm, vmem, vmem, vmem, hbm, vmem, hbm, vmem, smem],
        out_specs=(hbm, vmem, hbm, vmem),
        scratch_shapes=[
            low(2, 3, shard, width), low(2, shard, width), low(2, width, hidden), low(2, hidden, width),
            full(2, shard), full(1, hidden),
            low(rows, width), low(rows, width), low(rows, width), low(rows, width),
            *[low(heads, rows, HD) for _ in range(5)],
            *[low(heads, BLOCK, BLOCK * (i + 1)) for i in range(nblk)],
            *[low(BLOCK, BLOCK * (i + 1)) for i in range(nblk)],
            low(2, hidden, rows), low(2, rows, hidden), full(half, width), full(half, width),
            *[low(half, width) for _ in range(5)],
            low(total, width), low(2 * hidden, width), low(total, width), low(total // 2, width),
            low(3, total // 8, width), low(total // 8, width),
            pltpu.VMEM((rows, 1), jnp.int32),
            full(16, width), full(16, width), full(8, width), full(8, width),
            full(8, width), full(8, width), full(8, width), full(4, 8, width),
            dma((17,)), dma((17,)), dma((10,)), dma((10,)), dma((8,)), dma((8,)), dma((4,)),
            dma((CHUNKS,)), dma((CHUNKS,)), dma((CHUNKS,)), dma((CHUNKS,)),
            dma((3, CHUNKS)), dma((3, CHUNKS)), dma((3, CHUNKS)), dma((3, CHUNKS)),
            dma((CHUNKS,)), dma((CHUNKS,)), dma((CHUNKS + 1,)),
        ],
        compiler_params=pltpu.CompilerParams(
            collective_id=0, has_side_effects=True, vmem_limit_bytes=66_000_000
        ),
        name="block",
    )(
        inputs, cotangent, ln1_gain[None], ln1_bias[None], w_qkv.transpose(0, 2, 1), qv_bias, w_out, out_bias[None],
        ln2_gain[None], ln2_bias[None], w_fc, fc_bias[None], w_proj, proj_bias[None], doc_lengths,
    )
    layer_out, input_grad, grads, small = outs
    grads = grads.astype(F32)
    count = lax.axis_size("dp")
    if count > 8:
        groups = [[g * 8 + i for g in range(count // 8)] for i in range(8)]
        grads, small = lax.psum((grads, small), "dp", axis_index_groups=groups)
    proj_grad, fc_grad = grads[:hidden], grads[hidden:2 * hidden].T
    out_grad = grads[2 * hidden:2 * hidden + shard]
    qkv_grad = grads[2 * hidden + shard:].reshape(3, shard, width).transpose(0, 2, 1)
    qv_grad = jnp.stack([small[QVB, :shard], small[QVB, BLOCK:BLOCK + shard]])
    return (
        layer_out, input_grad, small[LN1G], small[LN1B], qkv_grad, qv_grad, out_grad, small[OUTB],
        small[LN2G], small[LN2B], fc_grad, small[FCB, :hidden], proj_grad, small[PROJB],
    )


def solution(mesh):
    tokens = P(("dp", "mp"), None)
    in_specs = (
        tokens, tokens, P(), P(), P(None, None, "mp"), P(None, "mp"), P("mp", None), P(), P(), P(),
        P(None, "mp"), P("mp"), P("mp", None), P(), P("dp", None),
    )
    out_specs = (
        tokens, tokens, P(), P(), P(None, None, "mp"), P(None, "mp"), P("mp", None), P(), P(), P(),
        P(None, "mp"), P("mp"), P("mp", None), P(),
    )
    return jax.shard_map(shards, mesh=mesh, in_specs=in_specs, out_specs=out_specs, check_vma=False)
```

```python
import math

import jax
import jax.numpy as jnp
from jax import lax
from jax.experimental import pallas as pl
from jax.experimental.pallas import tpu as pltpu
from jax.sharding import PartitionSpec as P

HD = 64
SCALE = 12 ** (-0.5)
MESH = pl.DeviceIdType.MESH
F32 = jnp.float32
BF16 = jnp.bfloat16
NN = (((1,), (0,)), ((), ()))
NT = (((1,), (1,)), ((), ()))
TN = (((0,), (0,)), ((), ()))
BLOCK = 256
LN1G, LN1B, OUTB, LN2G, LN2B, PROJB, FCB, QVB = range(8)
ORDERS = (
    ("y", "x", "z2", "z1"),
    ("z1", "y", "x", "z2"),
    ("x", "y", "z1", "z2"),
    ("z1", "y", "x", "z2"),
    ("x", "y", "z1", "z2"),
    ("z1", "y", "x", "z2"),
    ("z1", "y", "x", "z2"),
    ("x", "y", "z2", "z1"),
    ("y", "x", "z1", "z2"),
)
ROUTES = ("z1", "x", "z1", "x", "z1", "x", "z1", "x")
SENDS = (0, 1, 2, 3, 4, 5, 6, 7)
SCHEDULE = {
    "att0.0.0": (("w", 0, 0),),
    "att0.0.1": (("w", 1, 0),),
    "att0.3.1": (("w", 2, 0),),
    "att0.1.2": (("w", 0, 1),),
    "needqkv": (("w", 1, 1), ("w", 2, 1), ("w", 3, 0), ("w", 4, 0), ("w", 5, 0),),
    "att1.0.0": (("w", 3, 1), ("w", 6, 0),),
    "att1.0.1": (("w", 4, 1),),
    "att1.2.1": (("w", 7, 0),),
    "att1.3.2": (("w", 5, 1),),
    "ln2": (("w", 6, 1),),
    "feed0.2": (("w", 7, 1),),
    "mixb": (("g", 2, 0), ("g", 0, 0), ("g", 1, 0),),
    "gq1.0": (("g", 4, 0), ("g", 3, 0),),
    "gq0.0": (("g", 2, 1),),
    "ab1.1": (("g", 0, 1), ("g", 5, 0),),
    "gq0.1": (("g", 1, 1),),
    "ab0.2": (("g", 2, 2), ("g", 4, 1),),
    "mlpa.0": (("g", 6, 0), ("g", 3, 1),),
    "mlpa.1": (("g", 1, 2),),
    "ln1b.0": (("g", 0, 2),),
    "ln1b.1": (("g", 2, 3), ("g", 5, 1), ("g", 7, 0), ("g", 4, 2),),
    "mlpb.0": (("g", 3, 2), ("g", 1, 3), ("g", 0, 3),),
    "mlpb.2": (("s", 0),),
    "out": (("g", 5, 2),),
    "end": (("g", 2, 4), ("g", 4, 3), ("g", 8, 0), ("g", 0, 4), ("g", 3, 3), ("g", 2, 5), ("g", 1, 4), ("g", 6, 1), ("g", 5, 3), ("g", 8, 1), ("g", 4, 4), ("g", 7, 1), ("s", 1), ("g", 2, 6), ("g", 8, 2), ("g", 0, 5), ("g", 1, 5), ("g", 4, 5), ("g", 3, 4), ("g", 6, 2), ("s", 2), ("g", 5, 4), ("g", 0, 6), ("g", 7, 2), ("g", 1, 6), ("g", 8, 3), ("s", 3), ("g", 4, 6), ("g", 7, 3), ("g", 6, 3), ("g", 3, 5), ("g", 8, 4), ("g", 7, 4), ("g", 5, 5), ("s", 4), ("g", 6, 4), ("g", 3, 6), ("g", 8, 5), ("g", 6, 5), ("g", 7, 5), ("g", 5, 6), ("g", 8, 6), ("g", 6, 6), ("g", 7, 6),),
}


def dot(a, b, dims=NN):
    return lax.dot_general(a, b, dims, preferred_element_type=F32)


def rows_of(start, size, align=16):
    return pl.ds(pl.multiple_of(start, align), size)


def centre(values):
    average = jnp.mean(values, axis=-1, keepdims=True)
    centred = values - average
    spread = jnp.mean(centred * centred, axis=-1, keepdims=True)
    rate = lax.rsqrt(spread + 1e-05)
    return centred * rate, rate


def norm_back(grad, gain, normal, rate):
    n = grad * gain
    return rate * (n - jnp.mean(n, axis=-1, keepdims=True) - normal * jnp.mean(n * normal, axis=-1, keepdims=True))


def line(ref):
    return ref[...].reshape(1, -1)


def block_kernel(
    x_ref, cot_ref, g1, b1, wqkv_hbm, qvb, wout_hbm, ob, g2, b2, wfc_hbm, fcb, wproj_hbm, pb, docs,
    layer_out, input_grad, f_proj, f_fc, f_att, small_out,
    wqkv, wout, wfc, wproj, qvb_o, fcb_o, n1, n2, mg, ag, qh, kh, vh, mxh, mgh, p0, p1, p2, p3,
    s0, s1, s2, s3, dq, act_t, plo, hid, hg, send_a, r_attn, r_n2,
    g_own, g_oth, r_buf, lo, sm_a, sm_b, sm_c, sm_r,
    cs, cr, ws, wr, ls, gs, gr, ks,
):
    half, width = x_ref.shape
    rows = 2 * half
    shard = wout_hbm.shape[0]
    nh = shard // HD
    hidden = wproj_hbm.shape[0]
    nblk = rows // BLOCK
    hblk = half // BLOCK
    dp, mp = lax.axis_index("dp"), lax.axis_index("mp")
    core, y = lax.rem(mp, 2), lax.div(mp, 2)
    bits = {
        "y": y,
        "x": lax.rem(dp, 2),
        "z1": lax.rem(lax.div(dp, 2), 2),
        "z2": lax.rem(lax.div(dp, 4), 2),
    }
    targets = {
        "core": (dp, mp + 1 - 2 * core),
        "y": (dp, mp + 2 - 4 * y),
        "x": (dp + 1 - 2 * bits["x"], mp),
        "z1": (dp + 2 - 4 * bits["z1"], mp),
        "z2": (dp + 4 - 8 * bits["z2"], mp),
    }
    mine, theirs = core * half, (1 - core) * half
    probs, scores_grad = (p0, p1, p2, p3), (s0, s1, s2, s3)

    def remote(src, dst, send, recv, axis):
        return pltpu.make_async_remote_copy(
            src_ref=src, dst_ref=dst, send_sem=send, recv_sem=recv, device_id=targets[axis], device_id_type=MESH
        )

    def to_core(i, src, dst):
        return remote(src, dst, cs.at[i], cr.at[i], "core")

    barrier = pltpu.get_barrier_semaphore()
    for target in targets.values():
        pl.semaphore_signal(barrier, inc=1, device_id=target, device_id_type=MESH)
    pl.semaphore_wait(barrier, len(targets))

    group = bits["x"] + 2 * bits["z1"]
    beside = {"x": group + 1 - 2 * bits["x"], "z1": group + 2 - 4 * bits["z1"]}

    def slot_piece(ref, lead, j, index):
        if j < 3:
            return ref.at[(*lead, j, rows_of(index * (shard // 4), shard // 4))]
        if j == 3:
            return ref.at[(*lead, rows_of(index * (shard // 4), shard // 4))]
        size = width // 8
        return ref.at[(*lead, rows_of((j % 2) * 4 * size + index * size, size))]

    def slot_refs(j):
        if j < 3:
            return wqkv_hbm, wqkv
        if j == 3:
            return wout_hbm, wout
        return (wfc_hbm, wfc) if j < 6 else (wproj_hbm, wproj)

    def weight_copy(j, way):
        hbm, vmem = slot_refs(j)
        number = ("y", "x", "z1", "last").index(way)
        if way == "y":
            src, dst, axis = slot_piece(hbm, (), j, group), slot_piece(vmem, (1,), j, group), "y"
        else:
            axis = ROUTES[j] if way == "last" else way
            index = group if way != "last" else beside["x" if axis == "z1" else "z1"]
            src = dst = slot_piece(vmem, (1,), j, index)
        return remote(src, dst, ws.at[number, j], wr.at[number, j], axis)

    def weight_own(i):
        hbm, vmem = ((wqkv_hbm, wqkv), (wout_hbm, wout), (wfc_hbm, wfc), (wproj_hbm, wproj))[i]
        return pltpu.make_async_copy(hbm, vmem.at[0], ls.at[i])

    copy_qvb = remote(qvb, qvb_o, ws.at[0, 8], wr.at[0, 8], "y")
    copy_fcb = remote(fcb, fcb_o, ws.at[0, 9], wr.at[0, 9], "y")
    arrived = set()

    def weight_step(j, hop):
        if hop == 0:
            weight_copy(j, "y").wait_recv()
            weight_copy(j, "x").start()
            weight_copy(j, "z1").start()
        else:
            way = "x" if ROUTES[j] == "z1" else "z1"
            weight_copy(j, way).wait_recv()
            arrived.add((j, way))
            weight_copy(j, "last").start()

    def need(slots):
        for j in slots:
            for way in ("x", "z1", "last"):
                if (j, way) not in arrived:
                    weight_copy(j, way).wait_recv()

    each = BLOCK + BLOCK // 2 + BLOCK // 4 + BLOCK // 8
    stages = []
    for k, order in enumerate(ORDERS):
        offset, size, at, whole, plan = k * BLOCK, BLOCK, k * each, True, []
        for axis in order:
            if axis == "y":
                plan.append((axis, offset, offset, size, at, False))
                at, whole = at + size, False
            else:
                size //= 2
                keep, give = offset + bits[axis] * size, offset + (1 - bits[axis]) * size
                plan.append((axis, keep, give, size, at, whole))
                at, offset = at + size * (2 if whole else 1), keep
        stages.append(plan)

    def grad_copies(k, stage, only=(True, True)):
        axis, _, give, size, at, whole = stages[k][stage]
        parts = []
        if axis != "y":
            parts.append((g_own, 0))
        if axis == "y" or whole:
            parts.append((g_oth, len(parts)))
        parts = [part for part in parts if only[part[0] is g_oth]]
        return [
            remote(
                ref.at[rows_of(give, size)], r_buf.at[rows_of(at + i * size, size)],
                gs.at[k, 2 * stage + i], gr.at[k, 2 * stage + i], axis,
            )
            for ref, i in parts
        ]

    results = (f_proj, f_fc, f_att)

    def result_rows(k, start, size):
        return results[k // 3].at[rows_of(start - (k // 3) * 3 * BLOCK, size)]

    def gather_plan(k):
        return [entry for entry in reversed(stages[k]) if entry[0] != "y"]

    def gather_copy(k, i):
        plan = gather_plan(k)
        start, size = plan[i][1], plan[i][3]
        src = g_own.at[rows_of(start, size)] if i == 0 else result_rows(k, start, size)
        return remote(src, result_rows(k, start, size), gs.at[k, 8 + i], gr.at[k, 8 + i], plan[i][0])

    def keep_copy(k):
        start, size = gather_plan(k)[0][1], gather_plan(k)[0][3]
        return pltpu.make_async_copy(g_own.at[rows_of(start, size)], result_rows(k, start, size), ks.at[k])

    def add(ref, start, size, at):
        step = min(size, BLOCK // 4)

        def body(m, _):
            here, there = rows_of(start + m * step, step), rows_of(at + m * step, step)
            ref[here, :] = (ref[here, :].astype(F32) + r_buf[there, :].astype(F32)).astype(BF16)
            return 0

        if size == step:
            body(0, 0)
        else:
            lax.fori_loop(0, size // step, body, 0)

    def grad_step(k, stage):
        if stage < len(stages[k]):
            axis, keep, _, size, at, whole = stages[k][stage]
            for copy in grad_copies(k, stage):
                copy.wait_recv()
            add(g_own, keep, size, at)
            if whole:
                add(g_oth, keep, size, at + size)
            if stage + 1 < len(stages[k]):
                for copy in grad_copies(k, stage + 1):
                    copy.start()
            else:
                keep_copy(k).start()
                gather_copy(k, 0).start()
        else:
            i = stage - len(stages[k])
            gather_copy(k, i).wait_recv()
            if i == 0:
                keep_copy(k).wait()
            if i < 2:
                gather_copy(k, i + 1).start()

    def grad_ready(k, other):
        for copy in grad_copies(k, 0, (not other, other)):
            copy.start()

    def ready_at(first, t, s):
        for i in range(3):
            if s == 1 or ORDERS[first + i][0] != "y":
                pl.when(t == i)(lambda i=i: grad_ready(first + i, s == 1))

    ways = ("core", "y", "x", "z1", "z2")

    def small_copy(i):
        src = (sm_a.at[pl.ds(0, 8)], sm_b.at[pl.ds(8, 8)], sm_c.at[0], sm_c.at[1], sm_c.at[2])[i]
        return remote(src, sm_r.at[i], cs.at[11 + i], cr.at[11 + i], ways[i])

    def small_step(i):
        small_copy(i).wait()
        if i == 0:
            shared = lax.broadcasted_iota(jnp.int32, (8, width), 0) < FCB
            own, other = sm_a[pl.ds(0, 8), :], sm_a[pl.ds(8, 8), :]
            both = own + sm_r[0]
            sm_b[pl.ds(0, 8), :] = jnp.where(shared, both, own)
            sm_b[pl.ds(8, 8), :] = jnp.where(shared, both, other)
        elif i < 4:
            sm_c[i - 1] = (sm_b[pl.ds(0, 8), :] if i == 1 else sm_c[i - 2]) + sm_r[i]
        else:
            small_out[...] = sm_c[2] + sm_r[4]
        if i < 4:
            small_copy(i + 1).start()

    def service(point):
        for kind, *where in SCHEDULE.get(point, ()):
            {"w": weight_step, "g": grad_step, "s": small_step}[kind](*where)

    def service_at(point, t, count):
        for i in range(count):
            if f"{point}.{i}" in SCHEDULE:
                pl.when(t == i)(lambda i=i: service(f"{point}.{i}"))

    weight_own(0).start()
    copy_qvb.start()
    for j in SENDS:
        weight_copy(j, "y").start()
    copy_fcb.start()
    for i in range(1, 4):
        weight_own(i).start()

    def n1_copy(i):
        view = n1.at[rows_of(mine + i * BLOCK, BLOCK)]
        return to_core(i, view, view)

    for i in range(hblk):
        here = pl.ds(i * BLOCK, BLOCK)
        normal, _ = centre(x_ref[here, :].astype(F32))
        n1[rows_of(mine + i * BLOCK, BLOCK), :] = (normal * line(g1) + line(b1)).astype(BF16)
        n1_copy(i).start()

    def project(s, start, blocks):
        bias = qvb if s == 0 else qvb_o

        def body(m, _):
            here = rows_of(start + m * BLOCK, BLOCK)
            tokens = n1[here, :]
            for j, out in enumerate((qh, kh, vh)):
                t = dot(tokens, wqkv[s, j], NT)
                if j == 0:
                    t = (t + bias[pl.ds(0, 1), :]) * (1.0 / math.sqrt(HD))
                elif j == 2:
                    t = t + bias[pl.ds(1, 1), :]
                t = t.astype(BF16)
                for h in range(nh):
                    out[s * nh + h, here, :] = t[:, h * HD:(h + 1) * HD]
            return 0

        lax.fori_loop(0, blocks, body, 0)

    def first_keys():
        place = lax.broadcasted_iota(jnp.int32, (rows, 1), 0)
        first = jnp.zeros((rows, 1), jnp.int32)
        end = 0
        slots = docs.shape[1]
        for i in range(slots):
            end = end + docs[y, i]
            first = jnp.where(place >= end, place if i == slots - 1 else end, first)
        lo[...] = first

    def attend(s):
        def head(t, _):
            h = s * nh + t
            for i in range(nblk):
                service_at(f"att{s}.{i}", t, nh)
                seen = BLOCK * (i + 1)
                here = pl.ds(BLOCK * i, BLOCK)
                score = dot(qh[h, here, :], kh[h, pl.ds(0, seen), :], NT)
                key = lax.broadcasted_iota(jnp.int32, (BLOCK, seen), 1)
                query = lax.broadcasted_iota(jnp.int32, (BLOCK, seen), 0) + BLOCK * i
                score = jnp.where((key >= lo[here, :]) & (key <= query), score, -1e30)
                peak = jnp.max(score, axis=-1, keepdims=True)
                exponent = jnp.exp(score - peak)
                scale = 1.0 / jnp.sum(exponent, axis=-1, keepdims=True)
                low = (exponent * scale).astype(BF16)
                probs[i][h] = low
                mxh[h, here, :] = dot(low, vh[h, pl.ds(0, seen), :]).astype(BF16)
            return 0

        lax.fori_loop(0, nh, head, 0)

    weight_own(0).wait()
    service("qkv0a")
    project(0, mine, hblk)
    service("qkv0b")
    for i in range(hblk):
        n1_copy(i).wait_recv()
    project(0, theirs, hblk)
    first_keys()
    attend(0)

    service("mg")
    mg_copy = to_core(2, mg.at[rows_of(mine, half)], mg.at[rows_of(mine, half)])
    total = jnp.zeros((1, width), F32)
    for i in range(hblk):
        values = cot_ref[pl.ds(i * BLOCK, BLOCK), :].astype(F32)
        mg[rows_of(mine + i * BLOCK, BLOCK), :] = (SCALE * values).astype(BF16)
        total = total + jnp.sum(values, axis=0, keepdims=True)
    mg_copy.start()
    sm_a[...] = jnp.zeros_like(sm_a)
    sm_a[pl.ds(PROJB, 1), :] = SCALE * total

    service("needqkv")
    copy_qvb.wait_recv()
    need(range(3))
    service("qkv1a")
    project(1, 0, hblk)
    service("qkv1b")
    project(1, half, hblk)
    attend(1)

    service("needout")
    weight_own(1).wait()
    need(range(3, 4))

    def mixed_of(s, here):
        return jnp.concatenate([mxh[s * nh + h, here, :] for h in range(nh)], axis=1)

    def attn_out(here):
        return dot(mixed_of(0, here), wout[0]) + dot(mixed_of(1, here), wout[1])

    attn_copy = to_core(3, send_a, r_attn)

    def attn_theirs(m, _):
        send_a[rows_of(m * BLOCK, BLOCK), :] = attn_out(rows_of(theirs + m * BLOCK, BLOCK)).astype(BF16)
        return 0

    def attn_mine(m, _):
        here = rows_of(m * BLOCK, BLOCK)
        part = attn_out(rows_of(mine + m * BLOCK, BLOCK))
        hid[here, :] = x_ref[here, :].astype(F32) + SCALE * (part + line(ob))
        return 0

    service("outa")
    lax.fori_loop(0, hblk, attn_theirs, 0)
    attn_copy.start()
    service("outb")
    lax.fori_loop(0, hblk, attn_mine, 0)
    attn_copy.wait()

    def n2_copy(i):
        view = n2.at[rows_of(mine + i * BLOCK, BLOCK)]
        return to_core(4 + i, view, view)

    for i in range(hblk):
        here = pl.ds(i * BLOCK, BLOCK)
        state = hid[here, :] + SCALE * r_attn[here, :].astype(F32)
        hid[here, :] = state
        normal, _ = centre(state)
        n2[rows_of(mine + i * BLOCK, BLOCK), :] = (normal * line(g2) + line(b2)).astype(BF16)
        n2_copy(i).start()

    def feed(s):
        bias = line(fcb if s == 0 else fcb_o)
        a, b = math.sqrt(2 / math.pi), math.sqrt(2 / math.pi) * 0.044715
        out = g_own if s == 0 else g_oth

        def tile(f, _):
            service_at(f"feed{s}", f, hidden // BLOCK)
            cols = rows_of(f * BLOCK, BLOCK, BLOCK)
            total = jnp.zeros((1, BLOCK), F32)
            for m in range(2):
                here = pl.ds(half * m, half)
                u = dot(n2[here, :], wfc[s, :, cols]) + (fcb if s == 0 else fcb_o)[cols].reshape(1, -1)
                up = dot(mg[here, :], wproj[s, cols, :], NT)
                square = u * u
                th = jnp.tanh(u * (a + b * square))
                low = 0.5 + 0.5 * th
                act_t[s, cols, here] = (u * low).astype(BF16).T
                back = up * (low + (0.5 * u) * (1.0 - th * th) * (a + 3.0 * b * square))
                plo[s, here, cols] = back.astype(BF16)
                total = total + jnp.sum(back, axis=0, keepdims=True)
            sm_a[pl.ds(FCB + 8 * s, 1), cols] = total
            out[rows_of(f * BLOCK, BLOCK), :] = dot(act_t[s, cols, :], mg[...]).astype(BF16)
            ready_at(0, f, s)
            return 0

        lax.fori_loop(0, hidden // BLOCK, tile, 0)

    def grad_fc(s):
        out = g_own if s == 0 else g_oth

        def tile(n, _):
            service_at(f"gfc{s}", n, width // BLOCK)
            cols = rows_of(n * BLOCK, BLOCK, BLOCK)
            out[rows_of(hidden + n * BLOCK, BLOCK), :] = dot(n2[:, cols], plo[s], TN).astype(BF16)
            ready_at(3, n, s)
            return 0

        lax.fori_loop(0, width // BLOCK, tile, 0)

    service("ln2")
    for i in range(hblk):
        n2_copy(i).wait_recv()
    mg_copy.wait_recv()
    weight_own(2).wait()
    weight_own(3).wait()
    feed(0)
    grad_fc(0)
    service("needfp")
    copy_fcb.wait_recv()
    need(range(4, 8))
    feed(1)

    def norm2_part(here, cols):
        return dot(plo[0, here, :], wfc[0, cols, :], NT) + dot(plo[1, here, :], wfc[1, cols, :], NT)

    def norm2_theirs(n, _):
        cols = rows_of(n * BLOCK, BLOCK, BLOCK)
        send_a[:, cols] = norm2_part(rows_of(theirs, half), cols).astype(BF16)
        return 0

    def norm2_mine(n, _):
        cols = rows_of(n * BLOCK, BLOCK, BLOCK)
        hg[:, cols] = norm2_part(rows_of(mine, half), cols)
        return 0

    norm2_copy = to_core(7, send_a, r_n2)
    service("n2a")
    lax.fori_loop(0, width // BLOCK, norm2_theirs, 0)
    norm2_copy.start()
    service("n2b")
    lax.fori_loop(0, width // BLOCK, norm2_mine, 0)
    grad_fc(1)
    service("ln2b")
    norm2_copy.wait()

    def ag_copy(i):
        view = ag.at[rows_of(mine + i * BLOCK, BLOCK)]
        return to_core(8 + i, view, view)

    sums = [jnp.zeros((1, width), F32) for _ in range(3)]
    for i in range(hblk):
        here = pl.ds(i * BLOCK, BLOCK)
        grad = hg[here, :] + r_n2[here, :].astype(F32)
        normal, rate = centre(hid[here, :])
        state_grad = cot_ref[here, :].astype(F32) + norm_back(grad, line(g2), normal, rate)
        hg[here, :] = state_grad
        ag[rows_of(mine + i * BLOCK, BLOCK), :] = (SCALE * state_grad).astype(BF16)
        ag_copy(i).start()
        for j, value in enumerate((grad * normal, grad, SCALE * state_grad)):
            sums[j] = sums[j] + jnp.sum(value, axis=0, keepdims=True)
    sm_a[pl.ds(LN2G, 1), :] = sums[0]
    sm_a[pl.ds(LN2B, 1), :] = sums[1]
    sm_a[pl.ds(OUTB, 1), :] = sums[2]

    def mixed_grad(start):
        def body(m, _):
            here = rows_of(start + m * BLOCK, BLOCK)
            tokens = ag[here, :]
            for s in range(2):
                t = dot(tokens, wout[s], NT).astype(BF16)
                for h in range(nh):
                    mgh[s * nh + h, here, :] = t[:, h * HD:(h + 1) * HD]
            return 0

        lax.fori_loop(0, hblk, body, 0)

    service("mixa")
    mixed_grad(mine)
    for i in range(hblk):
        ag_copy(i).wait_recv()
    service("mixb")
    mixed_grad(theirs)

    def grad_out(s):
        out = g_own if s == 0 else g_oth

        def tile(n, _):
            cols = rows_of(n * BLOCK, BLOCK, BLOCK)
            product = dot(mixed_of(s, slice(None)), ag[:, cols], TN).astype(BF16)
            for h in range(nh):
                out[pl.ds(2 * hidden + h * BLOCK, HD), cols] = product[h * HD:(h + 1) * HD]
            return 0

        lax.fori_loop(0, width // BLOCK, tile, 0)

    service("gout")
    grad_out(1)
    grad_out(0)

    def head_back(s, t):
        h = s * nh + t
        first = rows_of(t * BLOCK, BLOCK, BLOCK)
        grad_t, query_t = mgh[h].T, qh[h].T
        for i in range(nblk):
            seen = BLOCK * (i + 1)
            here = pl.ds(BLOCK * i, BLOCK)
            d = mgh[h, here, :]
            inner = jnp.sum(d.astype(F32) * mxh[h, here, :].astype(F32), axis=-1, keepdims=True)
            prob_grad = dot(d, vh[h, pl.ds(0, seen), :], NT)
            ds = (probs[i][h].astype(F32) * (prob_grad - inner)).astype(BF16)
            scores_grad[i][...] = ds
            dq[here, :] = (dot(ds, kh[h, pl.ds(0, seen), :]) * (1.0 / math.sqrt(HD))).astype(BF16)
        for j in range(nblk):
            cols = pl.ds(BLOCK * j, BLOCK)
            value_grad = key_grad = 0.0
            for i in range(j, nblk):
                there = slice(BLOCK * i, BLOCK * (i + 1))
                value_grad = value_grad + dot(grad_t[:, there], probs[i][h, :, cols])
                key_grad = key_grad + dot(query_t[:, there], scores_grad[i][:, cols])
            pair = jnp.concatenate([key_grad, value_grad], axis=0).astype(BF16).T
            filler = jnp.zeros((BLOCK, HD), BF16)
            plo[s, cols, first] = jnp.concatenate([dq[cols, :], pair, filler], axis=1)

    def head_weights(s, t):
        out = g_own if s == 0 else g_oth
        cols = rows_of(t * BLOCK, BLOCK, BLOCK)
        product = dot(plo[s, :, cols], n1[...], TN)
        out[rows_of(2 * hidden + t * BLOCK + HD, 3 * HD), :] = product[:3 * HD].astype(BF16)

    def back(t, _):
        for s in (1, 0):
            service_at(f"ab{s}", t, nh)
            head_back(s, t)
            service_at(f"gq{s}", t, nh)
            head_weights(s, t)
            ready_at(6, t, s)
        return 0

    lax.fori_loop(0, nh, back, 0)

    def norm1_part(here):
        total = None
        for s in range(2):
            for h in range(nh):
                t = plo[s, here, pl.ds(h * BLOCK, 3 * HD)]
                spot = (pl.ds(QVB + 8 * s, 1), pl.ds(h * BLOCK, 3 * HD))
                sm_a[spot] = sm_a[spot] + jnp.sum(t.astype(F32), axis=0, keepdims=True)
                weights = jnp.concatenate([wqkv[s, j, pl.ds(h * HD, HD), :] for j in range(3)], axis=0)
                product = dot(t, weights)
                total = product if total is None else total + product
        return total

    def norm1_theirs(m, _):
        service_at("n1", m, hblk)
        here = rows_of(theirs + m * BLOCK, BLOCK)
        mg[here, :] = norm1_part(here).astype(BF16)
        return 0

    norm1_copy = to_core(10, mg.at[rows_of(theirs, half)], r_attn)
    lax.fori_loop(0, hblk, norm1_theirs, 0)
    norm1_copy.start()

    def mlp_part(here, cols):
        return dot(act_t[0, :, here], wproj[0, :, cols], TN) + dot(act_t[1, :, here], wproj[1, :, cols], TN)

    def mlp_theirs(n, _):
        service_at("mlpa", n, width // BLOCK)
        cols = rows_of(n * BLOCK, BLOCK, BLOCK)
        send_a[:, cols] = mlp_part(rows_of(theirs, half, BLOCK), cols).astype(BF16)
        return 0

    def mlp_mine(n, _):
        service_at("mlpb", n, width // BLOCK)
        cols = rows_of(n * BLOCK, BLOCK, BLOCK)
        hid[:, cols] = hid[:, cols] + SCALE * (mlp_part(rows_of(mine, half, BLOCK), cols) + pb[cols].reshape(1, -1))
        return 0

    mlp_copy = to_core(6, send_a, r_n2)
    lax.fori_loop(0, width // BLOCK, mlp_theirs, 0)
    mlp_copy.start()

    norm1_copy.wait()
    sums = [jnp.zeros((1, width), F32) for _ in range(2)]
    for i in range(hblk):
        service(f"ln1b.{i}")
        here = pl.ds(i * BLOCK, BLOCK)
        grad = norm1_part(rows_of(mine + i * BLOCK, BLOCK)) + r_attn[here, :].astype(F32)
        normal, rate = centre(x_ref[here, :].astype(F32))
        n1_copy(i).wait_send()
        n1[rows_of(mine + i * BLOCK, BLOCK), :] = (hg[here, :] + norm_back(grad, line(g1), normal, rate)).astype(BF16)
        sums[0] = sums[0] + jnp.sum(grad * normal, axis=0, keepdims=True)
        sums[1] = sums[1] + jnp.sum(grad, axis=0, keepdims=True)
    sm_a[pl.ds(LN1G, 1), :] = sums[0]
    sm_a[pl.ds(LN1B, 1), :] = sums[1]
    input_result = pltpu.make_async_copy(n1.at[rows_of(mine, half)], input_grad, ks.at[len(ORDERS) + 1])
    input_result.start()
    small_copy(0).start()

    lax.fori_loop(0, width // BLOCK, mlp_mine, 0)
    mlp_copy.wait()
    service("out")
    for i in range(hblk):
        n2_copy(i).wait_send()
        here = pl.ds(i * BLOCK, BLOCK)
        there = rows_of(mine + i * BLOCK, BLOCK)
        n2[there, :] = (hid[here, :] + SCALE * r_n2[here, :].astype(F32)).astype(BF16)
    result = pltpu.make_async_copy(n2.at[rows_of(mine, half)], layer_out, ks.at[len(ORDERS)])
    result.start()

    service("end")
    for k in range(len(ORDERS)):
        for stage in range(len(stages[k])):
            for copy in grad_copies(k, stage):
                copy.wait_send()
        for i in range(3):
            gather_copy(k, i).wait_send()
    for j in range(8):
        for way in ("y", "x", "z1", "last"):
            weight_copy(j, way).wait_send()
    for copy in (copy_qvb, copy_fcb, mg_copy):
        copy.wait_send()
    for i in range(hblk):
        ag_copy(i).wait_send()
    result.wait()
    input_result.wait()


def shards(
    inputs, cotangent, ln1_gain, ln1_bias, w_qkv, qv_bias, w_out, out_bias, ln2_gain, ln2_bias,
    w_fc, fc_bias, w_proj, proj_bias, doc_lengths,
):
    half, width = inputs.shape
    rows = 2 * half
    shard = w_out.shape[0]
    nh = shard // HD
    heads = 2 * nh
    hidden = w_proj.shape[0]
    nblk = rows // BLOCK
    count = len(ORDERS)
    vmem = pl.BlockSpec(memory_space=pltpu.VMEM)
    hbm = pl.BlockSpec(memory_space=pl.ANY)
    smem = pl.BlockSpec(memory_space=pltpu.SMEM)

    def low(*shape):
        return pltpu.VMEM(shape, BF16)

    def full(*shape):
        return pltpu.VMEM(shape, F32)

    dma = pltpu.SemaphoreType.DMA
    square = jax.ShapeDtypeStruct((hidden, width), BF16)
    layer_out, input_grad, proj, fc, att, small = pl.pallas_call(
        block_kernel,
        out_shape=(
            jax.ShapeDtypeStruct((half, width), BF16),
            jax.ShapeDtypeStruct((half, width), BF16),
            square, square, square,
            jax.ShapeDtypeStruct((8, width), F32),
        ),
        in_specs=[vmem, vmem, vmem, vmem, hbm, vmem, hbm, vmem, vmem, vmem, hbm, vmem, hbm, vmem, smem],
        out_specs=(hbm, hbm, hbm, hbm, hbm, vmem),
        scratch_shapes=[
            low(2, 3, shard, width), low(2, shard, width), low(2, width, hidden), low(2, hidden, width),
            full(2, shard), full(hidden),
            low(rows, width), low(rows, width), low(rows, width), low(rows, width),
            *[low(heads, rows, HD) for _ in range(5)],
            *[low(heads, BLOCK, BLOCK * (i + 1)) for i in range(nblk)],
            *[low(BLOCK, BLOCK * (i + 1)) for i in range(nblk)],
            low(rows, HD), low(2, hidden, rows), low(2, rows, hidden), full(half, width), full(half, width),
            *[low(half, width) for _ in range(3)],
            low(count * BLOCK, width), low(count * BLOCK, width), low(count * BLOCK // 8 * 15, width),
            pltpu.VMEM((rows, 1), jnp.int32),
            full(16, width), full(16, width), full(3, 8, width), full(5, 8, width),
            dma((16,)), dma((16,)), dma((4, 10)), dma((4, 10)), dma((4,)),
            dma((count, 11)), dma((count, 11)), dma((count + 2,)),
        ],
        compiler_params=pltpu.CompilerParams(
            collective_id=0, has_side_effects=True, vmem_limit_bytes=66_500_000
        ),
        name="block",
    )(
        inputs, cotangent, ln1_gain, ln1_bias, w_qkv.transpose(0, 2, 1), qv_bias, w_out, out_bias,
        ln2_gain, ln2_bias, w_fc, fc_bias, w_proj, proj_bias, doc_lengths,
    )
    devices = lax.axis_size("dp")
    if devices > 8:
        groups = [[g * 8 + i for g in range(devices // 8)] for i in range(8)]
        proj, fc, att, small = lax.psum(
            (proj.astype(F32), fc.astype(F32), att.astype(F32), small), "dp", axis_index_groups=groups
        )
    heads_first = att.reshape(nh, 4, HD, width)
    out_grad = heads_first[:, 0].reshape(shard, width).astype(F32)
    qkv_grad = heads_first[:, 1:].transpose(1, 0, 2, 3).reshape(3, shard, width).astype(F32).transpose(0, 2, 1)
    by_head = small[QVB].reshape(nh, BLOCK)
    qv_grad = jnp.stack([by_head[:, :HD].reshape(shard), by_head[:, 2 * HD:3 * HD].reshape(shard)])
    return (
        layer_out, input_grad, small[LN1G], small[LN1B], qkv_grad, qv_grad, out_grad, small[OUTB],
        small[LN2G], small[LN2B], fc.astype(F32), small[FCB], proj.astype(F32), small[PROJB],
    )


def solution(mesh):
    tokens = P(("dp", "mp"), None)
    in_specs = (
        tokens, tokens, P(), P(), P(None, None, "mp"), P(None, "mp"), P("mp", None), P(), P(), P(),
        P(None, "mp"), P("mp"), P("mp", None), P(), P("dp", None),
    )
    out_specs = (
        tokens, tokens, P(), P(), P(None, None, "mp"), P(None, "mp"), P("mp", None), P(), P(), P(),
        P(None, "mp"), P("mp"), P("mp", None), P(),
    )
    return jax.shard_map(shards, mesh=mesh, in_specs=in_specs, out_specs=out_specs, check_vma=False)
```

```python
import math

import jax
import jax.numpy as jnp
from jax import lax
from jax.experimental import pallas as pl
from jax.experimental.pallas import tpu as pltpu
from jax.sharding import PartitionSpec as P

HD = 64
SCALE = 12 ** (-0.5)
MESH = pl.DeviceIdType.MESH
F32 = jnp.float32
BF16 = jnp.bfloat16
NN = (((1,), (0,)), ((), ()))
NT = (((1,), (1,)), ((), ()))
TN = (((0,), (0,)), ((), ()))
BLOCK = 256
LN1G, LN1B, OUTB, LN2G, LN2B, PROJB, FCB, QVB = range(8)
CHUNKS = (
    (0, 0, 1, ("y", "x", "z1", "z2")),
    (1, 0, 1, ("x", "z", "y")),
    (2, 0, 1, ("z1", "y", "x", "z2")),
    (3, 0, 1, ("z1", "y", "x", "z2")),
    (4, 0, 1, ("x", "y", "z1", "z2")),
    (5, 0, 1, ("y", "x", "z1", "z2")),
    (6, 0, 1, ("x", "y", "z")),
    (7, 0, 1, ("y", "z1", "x", "z2")),
    (8, 0, 1, ("y", "x", "z")),
)
ROUTES = ("x", "x", "z1", "yx", "z1", "x", "z1", "y")
SCHEDULE = {
    "att0.1.0": (("w", 0, 0),),
    "att0.1.1": (("w", 1, 0),),
    "att0.3.1": (("w", 2, 0),),
    "att0.3.2": (("w", 0, 1),),
    "needqkv": (("w", 1, 1), ("w", 2, 1), ("w", 3, 0), ("w", 4, 0),),
    "qkv1b": (("w", 5, 0),),
    "att1.2.0": (("w", 6, 0),),
    "att1.2.1": (("w", 4, 1),),
    "att1.2.2": (("w", 5, 1),),
    "feed0.0": (("w", 6, 1),),
    "gfc0.0": (("g", 1, 0),),
    "ln2b": (("g", 2, 0), ("g", 0, 0),),
    "gq1.0": (("g", 4, 0),),
    "gq0.0": (("g", 5, 0),),
    "gq1.1": (("g", 0, 1), ("g", 1, 1),),
    "ab0.1": (("g", 2, 1),),
    "gq0.1": (("g", 3, 0),),
    "gq1.2": (("g", 4, 1), ("g", 0, 2),),
    "ab0.2": (("g", 1, 2),),
    "gq0.2": (("g", 5, 1),),
    "mlpa.0": (("g", 4, 2),),
    "mlpa.2": (("g", 6, 0), ("g", 0, 3),),
    "ln1b.1": (("g", 2, 2), ("g", 7, 0), ("g", 1, 3),),
    "mlpb.0": (("g", 5, 2),),
    "mlpb.2": (("g", 4, 3), ("g", 3, 1), ("s", 0),),
    "out": (("g", 0, 4),),
    "end": (
        ("g", 2, 3), ("g", 1, 4), ("g", 7, 1), ("g", 3, 2), ("g", 5, 3), ("g", 4, 4), ("g", 8, 0), ("g", 0, 5),
        ("g", 7, 2), ("g", 2, 4), ("g", 3, 3), ("g", 6, 1), ("s", 1), ("g", 5, 4), ("g", 4, 5), ("g", 8, 1),
        ("g", 7, 3), ("g", 3, 4), ("g", 0, 6), ("g", 2, 5), ("s", 2), ("g", 5, 5), ("g", 6, 2), ("g", 4, 6),
        ("g", 8, 2), ("g", 3, 5), ("g", 7, 4), ("g", 2, 6), ("s", 3), ("g", 5, 6), ("g", 7, 5), ("g", 6, 3),
        ("g", 8, 3), ("g", 3, 6), ("g", 6, 4), ("s", 4), ("g", 8, 4), ("g", 7, 6),
    ),
}


def dot(a, b, dims=NN):
    return lax.dot_general(a, b, dims, preferred_element_type=F32)


def rows_of(start, size, align=16):
    return pl.ds(pl.multiple_of(start, align), size)


def centre(values):
    average = jnp.mean(values, axis=-1, keepdims=True)
    centred = values - average
    spread = jnp.mean(centred * centred, axis=-1, keepdims=True)
    rate = lax.rsqrt(spread + 1e-05)
    return centred * rate, rate


def norm_back(grad, gain, normal, rate):
    n = grad * gain
    return rate * (n - jnp.mean(n, axis=-1, keepdims=True) - normal * jnp.mean(n * normal, axis=-1, keepdims=True))


def line(ref):
    return ref[...].reshape(1, -1)


def block_kernel(
    x_hbm, cot_hbm, g1, b1, wqkv_hbm, qvb, wout_hbm, ob, g2, b2, wfc_hbm, fcb, wproj_hbm, pb, docs,
    layer_out, input_grad, f_proj, f_fc, f_att, small_out,
    x_ref, cot_ref, wqkv, wout, wfc, wproj, qvb_o, fcb_o, n1, n2, mg, qh, kh, vh, mxh, mgh, p0, p1, p2, p3,
    s0, s1, s2, s3, dq, act_t, plo, hid, hg, send_a, r_attn, r_n2,
    g_own, g_oth, r_buf, lo, scales, sm_a, sm_b, sm_c, sm_r,
    cs, cr, ws, wr, ls, gs, gr, ks,
):
    half, width = x_hbm.shape
    rows = 2 * half
    shard = wout_hbm.shape[0]
    nh = shard // HD
    hidden = wproj_hbm.shape[0]
    nblk = rows // BLOCK
    hblk = half // BLOCK
    dp, mp = lax.axis_index("dp"), lax.axis_index("mp")
    core, y = lax.rem(mp, 2), lax.div(mp, 2)
    bits = {
        "y": y,
        "x": lax.rem(dp, 2),
        "z1": lax.rem(lax.div(dp, 2), 2),
        "z2": lax.rem(lax.div(dp, 4), 2),
    }
    zi = bits["z1"] + 2 * bits["z2"]
    targets = {
        "core": (dp, mp + 1 - 2 * core),
        "y": (dp, mp + 2 - 4 * y),
        "x": (dp + 1 - 2 * bits["x"], mp),
        "z1": (dp + 2 - 4 * bits["z1"], mp),
        "z2": (dp + 4 - 8 * bits["z2"], mp),
        "z3": (dp + 6 - 4 * zi, mp),
    }
    zs = {"z1": zi + 1 - 2 * bits["z1"], "z2": zi + 2 - 4 * bits["z2"], "z3": 3 - zi}
    mine, theirs = core * half, (1 - core) * half
    probs, scores_grad = (p0, p1, p2, p3), (s0, s1, s2, s3)

    def remote(src, dst, send, recv, axis):
        return pltpu.make_async_remote_copy(
            src_ref=src, dst_ref=dst, send_sem=send, recv_sem=recv, device_id=targets[axis], device_id_type=MESH
        )

    def to_core(i, src, dst):
        return remote(src, dst, cs.at[i], cr.at[i], "core")

    barrier = pltpu.get_barrier_semaphore()
    for target in targets.values():
        pl.semaphore_signal(barrier, inc=1, device_id=target, device_id_type=MESH)
    x_copy = pltpu.make_async_copy(x_hbm, x_ref, ls.at[4])
    cot_copy = pltpu.make_async_copy(cot_hbm, cot_ref, ls.at[5])
    x_copy.start()
    pl.semaphore_wait(barrier, len(targets))

    group = bits["x"] + 2 * bits["z1"]
    beside = {"x": group + 1 - 2 * bits["x"], "z1": group + 2 - 4 * bits["z1"]}

    def slot_piece(ref, lead, j, index, count=1):
        if j < 3:
            return ref.at[(*lead, j, rows_of(index * (shard // 4), count * (shard // 4)))]
        if j == 3:
            return ref.at[(*lead, rows_of(index * (shard // 4), count * (shard // 4)))]
        size = width // 8
        return ref.at[(*lead, rows_of((j % 2) * 4 * size + index * size, count * size))]

    def slot_refs(j):
        if j < 3:
            return wqkv_hbm, wqkv
        if j == 3:
            return wout_hbm, wout
        return (wfc_hbm, wfc) if j < 6 else (wproj_hbm, wproj)

    def ways_of(j):
        route = ROUTES[j]
        return ("y",) if route == "y" else ("y", "last") if route[0] == "y" else ("y", "x", "z1", "last")

    def weight_copy(j, way):
        hbm, vmem = slot_refs(j)
        route = ROUTES[j]
        axis = way if way != "last" else route[1:] if route[0] == "y" else route
        index, count = group, 1
        if route == "y":
            index, count = 0, 4
        elif route[0] == "y":
            index, count = 2 * bits[route[1:]], 2
        elif way == "last":
            index = beside["x" if axis == "z1" else "z1"]
        dst = slot_piece(vmem, (1,), j, index, count)
        src = slot_piece(hbm, (), j, index, count) if way == "y" else dst
        number = ("y", "x", "z1", "last").index(way)
        return remote(src, dst, ws.at[number, j], wr.at[number, j], axis)

    def weight_own(i):
        hbm, vmem = ((wqkv_hbm, wqkv), (wout_hbm, wout), (wfc_hbm, wfc), (wproj_hbm, wproj))[i]
        return pltpu.make_async_copy(hbm, vmem.at[0], ls.at[i])

    copy_qvb = remote(qvb, qvb_o, ws.at[0, 8], wr.at[0, 8], "y")
    copy_fcb = remote(fcb, fcb_o, ws.at[0, 9], wr.at[0, 9], "y")
    arrived = set()

    def weight_step(j, hop):
        if hop == 0:
            weight_copy(j, "y").wait_recv()
            arrived.add((j, "y"))
            for way in ways_of(j)[1:]:
                if way != "last" or ROUTES[j][0] == "y":
                    weight_copy(j, way).start()
        else:
            way = "x" if ROUTES[j] == "z1" else "z1"
            weight_copy(j, way).wait_recv()
            arrived.add((j, way))
            weight_copy(j, "last").start()

    def need(slots):
        for j in slots:
            for way in ways_of(j):
                if (j, way) not in arrived:
                    weight_copy(j, way).wait_recv()

    plans, at = [], 0
    for unit, part, parts, order in CHUNKS:
        size = BLOCK // parts
        offset, whole, plan = unit * BLOCK + part * size, True, []
        for axis in order:
            copies = []
            if axis == "y":
                whole = False
                copies.append(("y", True, offset, at))
                at += size
            else:
                size //= 4 if axis == "z" else 2
                place = zi if axis == "z" else bits[axis]
                for other in (False, True)[:2 if whole else 1]:
                    for way in ("z1", "z2", "z3") if axis == "z" else (axis,):
                        give = zs[way] if axis == "z" else 1 - place
                        copies.append((way, other, offset + give * size, at))
                        at += size
                offset = offset + place * size
            plan.append((axis, offset, size, copies))
        plans.append(plan)

    def grad_copy(k, stage, i):
        _, _, size, copies = plans[k][stage]
        way, other, start, there = copies[i]
        number = sum(len(entry[3]) for entry in plans[k][:stage]) + i
        return remote(
            (g_oth if other else g_own).at[rows_of(start, size)], r_buf.at[rows_of(there, size)],
            gs.at[k, number], gr.at[k, number], way,
        )

    results = (f_proj, f_fc, f_att)

    def result_rows(k, start, size):
        which = CHUNKS[k][0] // 3
        return results[which].at[rows_of(start - which * 3 * BLOCK, size)]

    def gather_plan(k):
        return [entry for entry in reversed(plans[k]) if entry[0] != "y"]

    def gather_copies(k, i):
        axis, start, size, _ = gather_plan(k)[i]
        src = g_own.at[rows_of(start, size)] if i == 0 else result_rows(k, start, size)
        ways = ("z1", "z2", "z3") if axis == "z" else (axis,)
        return [
            remote(src, result_rows(k, start, size), gs.at[k, 9 + 3 * i + n], gr.at[k, 9 + 3 * i + n], way)
            for n, way in enumerate(ways)
        ]

    def keep_copy(k):
        _, start, size, _ = gather_plan(k)[0]
        return pltpu.make_async_copy(g_own.at[rows_of(start, size)], result_rows(k, start, size), ks.at[k])

    def add(ref, start, size, sources):
        step = min(size, BLOCK // 4)

        def body(m, _):
            here = rows_of(start + m * step, step)
            total = ref[here, :]
            for there in sources:
                total = total + r_buf[rows_of(there + m * step, step), :]
            ref[here, :] = total
            return 0

        if size == step:
            body(0, 0)
        else:
            lax.fori_loop(0, size // step, body, 0)

    def grad_step(k, stage):
        if stage < len(plans[k]):
            axis, keep, size, copies = plans[k][stage]
            for i in range(len(copies)):
                grad_copy(k, stage, i).wait_recv()
            if axis == "y":
                add(g_own, keep, size, [copies[0][3]])
            else:
                for ref, other in ((g_own, False), (g_oth, True)):
                    sources = [copy[3] for copy in copies if copy[1] == other]
                    if sources:
                        add(ref, keep, size, sources)
            if stage + 1 < len(plans[k]):
                for i in range(len(plans[k][stage + 1][3])):
                    grad_copy(k, stage + 1, i).start()
            else:
                keep_copy(k).start()
                for copy in gather_copies(k, 0):
                    copy.start()
        else:
            i = stage - len(plans[k])
            for copy in gather_copies(k, i):
                copy.wait_recv()
            if i == 0:
                keep_copy(k).wait()
            if i + 1 < len(gather_plan(k)):
                for copy in gather_copies(k, i + 1):
                    copy.start()

    def unit_ready(unit, s):
        for k, chunk in enumerate(CHUNKS):
            if chunk[0] == unit:
                for i, copy in enumerate(plans[k][0][3]):
                    if copy[1] == (s == 1):
                        grad_copy(k, 0, i).start()

    def ready_at(first, t, s):
        for i in range(3):
            pl.when(t == i)(lambda i=i: unit_ready(first + i, s))

    ways = ("core", "y", "x", "z1", "z2")

    def small_copy(i):
        src = (sm_a.at[pl.ds(0, 8)], sm_b.at[pl.ds(8, 8)], sm_c.at[0], sm_c.at[1], sm_c.at[2])[i]
        return remote(src, sm_r.at[i], cs.at[11 + i], cr.at[11 + i], ways[i])

    def small_step(i):
        small_copy(i).wait()
        if i == 0:
            shared = lax.broadcasted_iota(jnp.int32, (8, width), 0) < FCB
            own, other = sm_a[pl.ds(0, 8), :], sm_a[pl.ds(8, 8), :]
            both = own + sm_r[0]
            sm_b[pl.ds(0, 8), :] = jnp.where(shared, both, own)
            sm_b[pl.ds(8, 8), :] = jnp.where(shared, both, other)
        elif i < 4:
            sm_c[i - 1] = (sm_b[pl.ds(0, 8), :] if i == 1 else sm_c[i - 2]) + sm_r[i]
        else:
            small_out[...] = sm_c[2] + sm_r[4]
        if i < 4:
            small_copy(i + 1).start()

    def service(point):
        for kind, *where in SCHEDULE.get(point, ()):
            {"w": weight_step, "g": grad_step, "s": small_step}[kind](*where)

    def service_at(point, t, count):
        for i in range(count):
            if f"{point}.{i}" in SCHEDULE:
                pl.when(t == i)(lambda i=i: service(f"{point}.{i}"))

    copy_qvb.start()
    for j in range(len(ROUTES)):
        weight_copy(j, "y").start()
    copy_fcb.start()
    for i in range(4):
        weight_own(i).start()
    cot_copy.start()
    scales[...] = jnp.zeros_like(scales)
    x_copy.wait()

    def n1_copy(i):
        view = n1.at[rows_of(mine + i * BLOCK, BLOCK)]
        return to_core(i, view, view)

    for i in range(hblk):
        here = pl.ds(i * BLOCK, BLOCK)
        normal, _ = centre(x_ref[here, :].astype(F32))
        n1[rows_of(mine + i * BLOCK, BLOCK), :] = (normal * line(g1) + line(b1)).astype(BF16)
        n1_copy(i).start()

    def project(s, start, blocks):
        bias = qvb if s == 0 else qvb_o

        def body(m, _):
            here = rows_of(start + m * BLOCK, BLOCK)
            tokens = n1[here, :]
            for j, out in enumerate((qh, kh, vh)):
                t = dot(tokens, wqkv[s, j], NT)
                if j == 0:
                    t = (t + bias[pl.ds(0, 1), :]) * (1.0 / math.sqrt(HD))
                elif j == 2:
                    t = t + bias[pl.ds(1, 1), :]
                t = t.astype(BF16)
                for h in range(nh):
                    out[s * nh + h, here, :] = t[:, h * HD:(h + 1) * HD]
            return 0

        lax.fori_loop(0, blocks, body, 0)

    def first_keys():
        place = lax.broadcasted_iota(jnp.int32, (rows, 1), 0)
        first = jnp.zeros((rows, 1), jnp.int32)
        end = 0
        slots = docs.shape[1]
        for i in range(slots):
            end = end + docs[y, i]
            first = jnp.where(place >= end, place if i == slots - 1 else end, first)
        lo[...] = first

    def attend(s):
        def head(t, _):
            h = s * nh + t
            values_t = vh[h].T
            for n in range(nblk):
                i = nblk - 1 - n
                service_at(f"att{s}.{n}", t, nh)
                here, before, seen = pl.ds(BLOCK * i, BLOCK), pl.ds(0, BLOCK * i), BLOCK * i
                first = lo[here, :]
                key = lax.broadcasted_iota(jnp.int32, (BLOCK, BLOCK), 1) + seen
                query = lax.broadcasted_iota(jnp.int32, (BLOCK, BLOCK), 0) + seen
                near = dot(qh[h, here, :], kh[h, here, :], NT)
                near = jnp.where((key >= first) & (key <= query), near, -1e30)
                peak = jnp.max(near, axis=-1, keepdims=True)
                if i:
                    far = dot(qh[h, here, :], kh[h, before, :], NT)
                    far = jnp.where(lax.broadcasted_iota(jnp.int32, (BLOCK, seen), 1) >= first, far, -1e30)
                    peak = jnp.maximum(peak, jnp.max(far, axis=-1, keepdims=True))
                near = jnp.exp(near - peak)
                total = jnp.sum(near, axis=-1, keepdims=True)
                near = near.astype(BF16)
                probs[i][h, :, here] = near
                mixed_t = dot(values_t[:, seen:seen + BLOCK], near, NT)
                if i:
                    far = jnp.exp(far - peak)
                    total = total + jnp.sum(far, axis=-1, keepdims=True)
                    far = far.astype(BF16)
                    probs[i][h, :, before] = far
                    mixed_t = mixed_t + dot(values_t[:, :seen], far, NT)
                scale = 1.0 / total
                mxh[h, here, :] = (mixed_t.T * scale).astype(BF16)
                lane = lax.broadcasted_iota(jnp.int32, (BLOCK, scales.shape[1]), 1)
                scales[here, :] = jnp.where(lane == h, scale, scales[here, :])
            return 0

        lax.fori_loop(0, nh, head, 0)

    weight_own(0).wait()
    service("qkv0a")
    project(0, mine, hblk)
    service("qkv0b")
    for i in range(hblk):
        n1_copy(i).wait_recv()
    project(0, theirs, hblk)
    first_keys()
    attend(0)

    service("mg")
    mg_copy = to_core(2, mg.at[rows_of(mine, half)], mg.at[rows_of(mine, half)])
    cot_copy.wait()
    total = jnp.zeros((1, width), F32)
    for i in range(hblk):
        values = cot_ref[pl.ds(i * BLOCK, BLOCK), :].astype(F32)
        mg[rows_of(mine + i * BLOCK, BLOCK), :] = (SCALE * values).astype(BF16)
        total = total + jnp.sum(values, axis=0, keepdims=True)
    mg_copy.start()
    sm_a[...] = jnp.zeros_like(sm_a)
    sm_a[pl.ds(PROJB, 1), :] = SCALE * total

    service("needqkv")
    copy_qvb.wait_recv()
    need(range(3))
    service("qkv1a")
    project(1, 0, hblk)
    service("qkv1b")
    project(1, half, hblk)
    attend(1)

    service("needout")
    weight_own(1).wait()
    need(range(3, 4))

    def mixed_of(s, here):
        return jnp.concatenate([mxh[s * nh + h, here, :] for h in range(nh)], axis=1)

    def attn_out(here):
        return dot(mixed_of(0, here), wout[0]) + dot(mixed_of(1, here), wout[1])

    attn_copy = to_core(3, send_a, r_attn)

    def attn_theirs(m, _):
        send_a[rows_of(m * BLOCK, BLOCK), :] = attn_out(rows_of(theirs + m * BLOCK, BLOCK)).astype(BF16)
        return 0

    def attn_mine(m, _):
        here = rows_of(m * BLOCK, BLOCK)
        part = attn_out(rows_of(mine + m * BLOCK, BLOCK))
        hid[here, :] = x_ref[here, :].astype(F32) + SCALE * (part + line(ob))
        return 0

    service("outa")
    lax.fori_loop(0, hblk, attn_theirs, 0)
    attn_copy.start()
    service("outb")
    lax.fori_loop(0, hblk, attn_mine, 0)
    attn_copy.wait()

    def n2_copy(i):
        view = n2.at[rows_of(mine + i * BLOCK, BLOCK)]
        return to_core(4 + i, view, view)

    for i in range(hblk):
        here = pl.ds(i * BLOCK, BLOCK)
        state = hid[here, :] + SCALE * r_attn[here, :].astype(F32)
        hid[here, :] = state
        normal, _ = centre(state)
        n2[rows_of(mine + i * BLOCK, BLOCK), :] = (normal * line(g2) + line(b2)).astype(BF16)
        n2_copy(i).start()

    def others_here():
        for i in range(hblk):
            n2_copy(i).wait_recv()
        mg_copy.wait_recv()

    def feed(s):
        a, b = math.sqrt(2 / math.pi), math.sqrt(2 / math.pi) * 0.044715
        out = g_own if s == 0 else g_oth

        def tile(f, _):
            service_at(f"feed{s}", f, hidden // BLOCK)
            cols = rows_of(f * BLOCK, BLOCK, BLOCK)
            total = jnp.zeros((1, BLOCK), F32)
            for m, start in enumerate((mine, theirs)):
                here = rows_of(start, half, half)
                if m == 1 and s == 0:
                    pl.when(f == 0)(others_here)
                u = dot(n2[here, :], wfc[s, :, cols]) + (fcb if s == 0 else fcb_o)[cols].reshape(1, -1)
                up = dot(mg[here, :], wproj[s, cols, :], NT)
                square = u * u
                th = jnp.tanh(u * (a + b * square))
                low = 0.5 + 0.5 * th
                act_t[s, cols, here] = (u * low).astype(BF16).T
                back = up * (low + (0.5 * u) * (1.0 - th * th) * (a + 3.0 * b * square))
                plo[s, here, cols] = back.astype(BF16)
                total = total + jnp.sum(back, axis=0, keepdims=True)
            sm_a[pl.ds(FCB + 8 * s, 1), cols] = total
            out[rows_of(f * BLOCK, BLOCK), :] = dot(act_t[s, cols, :], mg[...]).astype(BF16)
            ready_at(0, f, s)
            return 0

        lax.fori_loop(0, hidden // BLOCK, tile, 0)

    def grad_fc(s):
        out = g_own if s == 0 else g_oth

        def tile(n, _):
            service_at(f"gfc{s}", n, width // BLOCK)
            cols = rows_of(n * BLOCK, BLOCK, BLOCK)
            out[rows_of(hidden + n * BLOCK, BLOCK), :] = dot(n2[:, cols], plo[s], TN).astype(BF16)
            ready_at(3, n, s)
            return 0

        lax.fori_loop(0, width // BLOCK, tile, 0)

    service("ln2")
    weight_own(2).wait()
    weight_own(3).wait()
    feed(0)
    service("needfp")
    copy_fcb.wait_recv()
    need(range(4, 8))
    feed(1)
    grad_fc(1)

    def norm2_part(here, cols):
        return dot(plo[0, here, :], wfc[0, cols, :], NT) + dot(plo[1, here, :], wfc[1, cols, :], NT)

    def norm2_theirs(n, _):
        cols = rows_of(n * BLOCK, BLOCK, BLOCK)
        send_a[:, cols] = norm2_part(rows_of(theirs, half), cols).astype(BF16)
        return 0

    def norm2_mine(n, _):
        cols = rows_of(n * BLOCK, BLOCK, BLOCK)
        hg[:, cols] = norm2_part(rows_of(mine, half), cols)
        return 0

    norm2_copy = to_core(7, send_a, r_n2)
    service("n2a")
    lax.fori_loop(0, width // BLOCK, norm2_theirs, 0)
    norm2_copy.start()
    service("n2b")
    lax.fori_loop(0, width // BLOCK, norm2_mine, 0)
    grad_fc(0)
    service("ln2b")
    norm2_copy.wait()

    mg_copy.wait_send()

    def ag_copy(i):
        view = mg.at[rows_of(mine + i * BLOCK, BLOCK)]
        return to_core(8 + i, view, view)

    sums = [jnp.zeros((1, width), F32) for _ in range(3)]
    for i in range(hblk):
        here = pl.ds(i * BLOCK, BLOCK)
        grad = hg[here, :] + r_n2[here, :].astype(F32)
        normal, rate = centre(hid[here, :])
        state_grad = cot_ref[here, :].astype(F32) + norm_back(grad, line(g2), normal, rate)
        hg[here, :] = state_grad
        mg[rows_of(mine + i * BLOCK, BLOCK), :] = (SCALE * state_grad).astype(BF16)
        ag_copy(i).start()
        for j, value in enumerate((grad * normal, grad, SCALE * state_grad)):
            sums[j] = sums[j] + jnp.sum(value, axis=0, keepdims=True)
    sm_a[pl.ds(LN2G, 1), :] = sums[0]
    sm_a[pl.ds(LN2B, 1), :] = sums[1]
    sm_a[pl.ds(OUTB, 1), :] = sums[2]

    def mixed_grad(start):
        def body(m, _):
            here = rows_of(start + m * BLOCK, BLOCK)
            tokens = mg[here, :]
            for s in range(2):
                t = dot(tokens, wout[s], NT)
                for h in range(nh):
                    scale = scales[here, s * nh + h:s * nh + h + 1]
                    mgh[s * nh + h, here, :] = (t[:, h * HD:(h + 1) * HD] * scale).astype(BF16)
            return 0

        lax.fori_loop(0, hblk, body, 0)

    service("mixa")
    mixed_grad(mine)
    for i in range(hblk):
        ag_copy(i).wait_recv()
    service("mixb")
    mixed_grad(theirs)

    def grad_out(s):
        out = g_own if s == 0 else g_oth

        def tile(n, _):
            cols = rows_of(n * BLOCK, BLOCK, BLOCK)
            product = dot(mixed_of(s, slice(None)), mg[:, cols], TN).astype(BF16)
            for h in range(nh):
                out[pl.ds(2 * hidden + h * BLOCK, HD), cols] = product[h * HD:(h + 1) * HD]
            return 0

        lax.fori_loop(0, width // BLOCK, tile, 0)

    service("gout")
    grad_out(1)
    grad_out(0)

    def head_back(s, t):
        h = s * nh + t
        first = rows_of(t * BLOCK, BLOCK, BLOCK)
        grad_t, query_t = mgh[h].T, qh[h].T
        for i in range(nblk):
            seen = BLOCK * (i + 1)
            here = pl.ds(BLOCK * i, BLOCK)
            d = mgh[h, here, :]
            inner = jnp.sum(d.astype(F32) * mxh[h, here, :].astype(F32), axis=-1, keepdims=True)
            prob_grad = dot(d, vh[h, pl.ds(0, seen), :], NT)
            ds = (probs[i][h].astype(F32) * (prob_grad - inner)).astype(BF16)
            scores_grad[i][...] = ds
            dq[here, :] = (dot(ds, kh[h, pl.ds(0, seen), :]) * (1.0 / math.sqrt(HD))).astype(BF16)
        for j in range(nblk):
            cols = pl.ds(BLOCK * j, BLOCK)
            value_grad = key_grad = 0.0
            for i in range(j, nblk):
                there = slice(BLOCK * i, BLOCK * (i + 1))
                value_grad = value_grad + dot(grad_t[:, there], probs[i][h, :, cols])
                key_grad = key_grad + dot(query_t[:, there], scores_grad[i][:, cols])
            pair = jnp.concatenate([key_grad, value_grad], axis=0).astype(BF16).T
            filler = jnp.zeros((BLOCK, HD), BF16)
            plo[s, cols, first] = jnp.concatenate([dq[cols, :], pair, filler], axis=1)

    def head_weights(s, t):
        out = g_own if s == 0 else g_oth
        cols = rows_of(t * BLOCK, BLOCK, BLOCK)
        product = dot(plo[s, :, cols], n1[...], TN)
        out[rows_of(2 * hidden + t * BLOCK + HD, 3 * HD), :] = product[:3 * HD].astype(BF16)

    def back(t, _):
        for s in (1, 0):
            service_at(f"ab{s}", t, nh)
            head_back(s, t)
            service_at(f"gq{s}", t, nh)
            head_weights(s, t)
            ready_at(6, t, s)
        return 0

    lax.fori_loop(0, nh, back, 0)

    def norm1_part(here):
        total = None
        for s in range(2):
            for h in range(nh):
                t = plo[s, here, pl.ds(h * BLOCK, 3 * HD)]
                spot = (pl.ds(QVB + 8 * s, 1), pl.ds(h * BLOCK, 3 * HD))
                sm_a[spot] = sm_a[spot] + jnp.sum(t.astype(F32), axis=0, keepdims=True)
                weights = jnp.concatenate([wqkv[s, j, pl.ds(h * HD, HD), :] for j in range(3)], axis=0)
                product = dot(t, weights)
                total = product if total is None else total + product
        return total

    def norm1_theirs(m, _):
        service_at("n1", m, hblk)
        here = rows_of(theirs + m * BLOCK, BLOCK)
        mg[here, :] = norm1_part(here).astype(BF16)
        return 0

    norm1_copy = to_core(10, mg.at[rows_of(theirs, half)], r_attn)
    lax.fori_loop(0, hblk, norm1_theirs, 0)
    norm1_copy.start()

    def mlp_part(here, cols):
        return dot(act_t[0, :, here], wproj[0, :, cols], TN) + dot(act_t[1, :, here], wproj[1, :, cols], TN)

    def mlp_theirs(n, _):
        service_at("mlpa", n, width // BLOCK)
        cols = rows_of(n * BLOCK, BLOCK, BLOCK)
        send_a[:, cols] = mlp_part(rows_of(theirs, half, BLOCK), cols).astype(BF16)
        return 0

    def mlp_mine(n, _):
        service_at("mlpb", n, width // BLOCK)
        cols = rows_of(n * BLOCK, BLOCK, BLOCK)
        hid[:, cols] = hid[:, cols] + SCALE * (mlp_part(rows_of(mine, half, BLOCK), cols) + pb[cols].reshape(1, -1))
        return 0

    mlp_copy = to_core(6, send_a, r_n2)
    lax.fori_loop(0, width // BLOCK, mlp_theirs, 0)
    mlp_copy.start()

    norm1_copy.wait()
    sums = [jnp.zeros((1, width), F32) for _ in range(2)]
    for i in range(hblk):
        service(f"ln1b.{i}")
        here = pl.ds(i * BLOCK, BLOCK)
        grad = norm1_part(rows_of(mine + i * BLOCK, BLOCK)) + r_attn[here, :].astype(F32)
        normal, rate = centre(x_ref[here, :].astype(F32))
        n1_copy(i).wait_send()
        n1[rows_of(mine + i * BLOCK, BLOCK), :] = (hg[here, :] + norm_back(grad, line(g1), normal, rate)).astype(BF16)
        sums[0] = sums[0] + jnp.sum(grad * normal, axis=0, keepdims=True)
        sums[1] = sums[1] + jnp.sum(grad, axis=0, keepdims=True)
    sm_a[pl.ds(LN1G, 1), :] = sums[0]
    sm_a[pl.ds(LN1B, 1), :] = sums[1]
    input_result = pltpu.make_async_copy(n1.at[rows_of(mine, half)], input_grad, ks.at[len(CHUNKS) + 1])
    input_result.start()
    small_copy(0).start()

    lax.fori_loop(0, width // BLOCK, mlp_mine, 0)
    mlp_copy.wait()
    service("out")
    for i in range(hblk):
        n2_copy(i).wait_send()
        here = pl.ds(i * BLOCK, BLOCK)
        there = rows_of(mine + i * BLOCK, BLOCK)
        n2[there, :] = (hid[here, :] + SCALE * r_n2[here, :].astype(F32)).astype(BF16)
    result = pltpu.make_async_copy(n2.at[rows_of(mine, half)], layer_out, ks.at[len(CHUNKS)])
    result.start()

    service("end")
    for k in range(len(CHUNKS)):
        for stage in range(len(plans[k])):
            for i in range(len(plans[k][stage][3])):
                grad_copy(k, stage, i).wait_send()
        for i in range(len(gather_plan(k))):
            for copy in gather_copies(k, i):
                copy.wait_send()
    for j in range(len(ROUTES)):
        for way in ways_of(j):
            weight_copy(j, way).wait_send()
    for copy in (copy_qvb, copy_fcb):
        copy.wait_send()
    for i in range(hblk):
        ag_copy(i).wait_send()
    result.wait()
    input_result.wait()


def finish(
    proj_in, fc_in, att_in, layer_in, grad_in, small,
    proj_out, fc_out, out_out, qkv_out, layer_out, grad_out, ln1g, ln1b, outb, ln2g, ln2b, projb, fcb, qvb,
    proj_low, fc_low, att_low, layer_low, grad_low, proj_full, fc_full, out_full, qkv_full, sems,
):
    nh = out_out.shape[0] // HD
    loads = [
        pltpu.make_async_copy(src, dst, sems.at[i])
        for i, (src, dst) in enumerate(
            (
                (proj_in, proj_low), (fc_in, fc_low), (att_in, att_low), (layer_in, layer_low), (grad_in, grad_low),
            )
        )
    ]
    stores = [
        pltpu.make_async_copy(src, dst, sems.at[5 + i])
        for i, (src, dst) in enumerate(
            (
                (proj_full, proj_out), (fc_full, fc_out), (out_full, out_out), (qkv_full, qkv_out),
                (layer_low, layer_out), (grad_low, grad_out),
            )
        )
    ]
    for copy in loads:
        copy.start()
    for row, ref in ((LN1G, ln1g), (LN1B, ln1b), (OUTB, outb), (LN2G, ln2g), (LN2B, ln2b), (PROJB, projb), (FCB, fcb)):
        ref[...] = small[row, :]
    for i in range(2):
        cols = [slice(h * BLOCK + 2 * i * HD, h * BLOCK + (2 * i + 1) * HD) for h in range(nh)]
        qvb[pl.ds(i, 1), :] = jnp.concatenate([small[pl.ds(QVB, 1), c] for c in cols], axis=1)
    for i, (low, wide) in enumerate(((proj_low, proj_full), (fc_low, fc_full))):
        loads[i].wait()

        def body(m, _):
            here = rows_of(m * BLOCK, BLOCK)
            wide[here, :] = low[here, :].astype(F32)
            return 0

        lax.fori_loop(0, wide.shape[0] // BLOCK, body, 0)
        stores[i].start()
    for i in (3, 4):
        loads[i].wait()
        stores[i + 1].start()
    loads[2].wait()
    for h in range(nh):
        out_full[pl.ds(h * HD, HD), :] = att_low[pl.ds(h * BLOCK, HD), :].astype(F32)
        for j in range(3):
            qkv_full[j, pl.ds(h * HD, HD), :] = att_low[pl.ds(h * BLOCK + (j + 1) * HD, HD), :].astype(F32)
    stores[2].start()
    stores[3].start()
    for copy in stores:
        copy.wait()


def shards(
    inputs, cotangent, ln1_gain, ln1_bias, w_qkv, qv_bias, w_out, out_bias, ln2_gain, ln2_bias,
    w_fc, fc_bias, w_proj, proj_bias, doc_lengths,
):
    half, width = inputs.shape
    rows = 2 * half
    shard = w_out.shape[0]
    nh = shard // HD
    heads = 2 * nh
    hidden = w_proj.shape[0]
    nblk = rows // BLOCK
    count = len(CHUNKS)
    total = 2 * hidden + 4 * shard
    vmem = pl.BlockSpec(memory_space=pltpu.VMEM)
    hbm = pl.BlockSpec(memory_space=pl.ANY)
    smem = pl.BlockSpec(memory_space=pltpu.SMEM)

    def low(*shape):
        return pltpu.VMEM(shape, BF16)

    def full(*shape):
        return pltpu.VMEM(shape, F32)

    dma = pltpu.SemaphoreType.DMA
    square = jax.ShapeDtypeStruct((hidden, width), BF16)
    layer_out, input_grad, proj, fc, att, small = pl.pallas_call(
        block_kernel,
        out_shape=(
            jax.ShapeDtypeStruct((half, width), BF16),
            jax.ShapeDtypeStruct((half, width), BF16),
            square, square, square,
            jax.ShapeDtypeStruct((8, width), F32),
        ),
        in_specs=[hbm, hbm, vmem, vmem, hbm, vmem, hbm, vmem, vmem, vmem, hbm, vmem, hbm, vmem, smem],
        out_specs=(hbm, hbm, hbm, hbm, hbm, vmem),
        scratch_shapes=[
            low(half, width), low(half, width), low(2, 3, shard, width), low(2, shard, width), low(2, width, hidden), low(2, hidden, width),
            full(2, shard), full(hidden),
            low(rows, width), low(rows, width), low(rows, width),
            *[low(heads, rows, HD) for _ in range(5)],
            *[low(heads, BLOCK, BLOCK * (i + 1)) for i in range(nblk)],
            *[low(BLOCK, BLOCK * (i + 1)) for i in range(nblk)],
            low(rows, HD), low(2, hidden, rows), low(2, rows, hidden), full(half, width), full(half, width),
            *[low(half, width) for _ in range(3)],
            low(total, width), low(total, width), low(total // 8 * 15, width),
            pltpu.VMEM((rows, 1), jnp.int32), full(rows, 128),
            full(16, width), full(16, width), full(3, 8, width), full(5, 8, width),
            dma((16,)), dma((16,)), dma((4, 10)), dma((4, 10)), dma((6,)),
            dma((count, 18)), dma((count, 18)), dma((count + 2,)),
        ],
        compiler_params=pltpu.CompilerParams(
            collective_id=0, has_side_effects=True, vmem_limit_bytes=66_000_000
        ),
        name="block",
    )(
        inputs, cotangent, ln1_gain, ln1_bias, w_qkv.transpose(0, 2, 1), qv_bias, w_out, out_bias,
        ln2_gain, ln2_bias, w_fc, fc_bias, w_proj, proj_bias, doc_lengths,
    )
    devices = lax.axis_size("dp")
    if devices > 8:
        groups = [[g * 8 + i for g in range(devices // 8)] for i in range(8)]
        proj, fc, att, small = lax.psum(
            (proj.astype(F32), fc.astype(F32), att.astype(F32), small), "dp", axis_index_groups=groups
        )
    def vector(length):
        return jax.ShapeDtypeStruct((length,), F32)

    outs = pl.pallas_call(
        finish,
        out_shape=(
            jax.ShapeDtypeStruct((hidden, width), F32), jax.ShapeDtypeStruct((width, hidden), F32),
            jax.ShapeDtypeStruct((shard, width), F32), jax.ShapeDtypeStruct((3, shard, width), F32),
            jax.ShapeDtypeStruct((half, width), BF16), jax.ShapeDtypeStruct((half, width), BF16),
            *[vector(width) for _ in range(6)], vector(hidden), jax.ShapeDtypeStruct((2, shard), F32),
        ),
        in_specs=[hbm] * 5 + [vmem],
        out_specs=(hbm,) * 6 + (vmem,) * 8,
        scratch_shapes=[
            *[pltpu.VMEM(ref.shape, ref.dtype) for ref in (proj, fc, att, layer_out, input_grad)],
            full(hidden, width), full(width, hidden), full(shard, width), full(3, shard, width),
            dma((11,)),
        ],
        compiler_params=pltpu.CompilerParams(vmem_limit_bytes=60 << 20),
        name="finish",
    )(proj, fc, att, layer_out, input_grad, small)
    proj, fc, out, qkv, layer_out, input_grad, ln1g, ln1b, outb, ln2g, ln2b, projb, fcb, qvb = outs
    return (
        layer_out, input_grad, ln1g, ln1b, qkv.transpose(0, 2, 1), qvb, out, outb, ln2g, ln2b, fc, fcb, proj, projb,
    )


def solution(mesh):
    tokens = P(("dp", "mp"), None)
    in_specs = (
        tokens, tokens, P(), P(), P(None, None, "mp"), P(None, "mp"), P("mp", None), P(), P(), P(),
        P(None, "mp"), P("mp"), P("mp", None), P(), P("dp", None),
    )
    out_specs = (
        tokens, tokens, P(), P(), P(None, None, "mp"), P(None, "mp"), P("mp", None), P(), P(), P(),
        P(None, "mp"), P("mp"), P("mp", None), P(),
    )
    return jax.shard_map(shards, mesh=mesh, in_specs=in_specs, out_specs=out_specs, check_vma=False)
```
